256 devices in a mesh: pipe: 16 (over x_lo, y, core), ctx: 16 (over z, x_hi).
Axes of the slice: x: 4 (x_hi: 2, x_lo: 2; x = x_hi * 2 + x_lo), y: 4, z: 8, core: 2. Of those that a mesh axis runs over, the one named last changes fastest.
Arguments:
- queries: bfloat16 [16, 2048, 4096], P('pipe', 'ctx'), may hold values from -6 to 6
- key_heads: bfloat16 [16, 2048, 512], P('pipe', 'ctx'), may hold values from -6 to 6
- value_heads: bfloat16 [16, 2048, 512], P('pipe', 'ctx'), may hold values from -0.59765625 to 0.59765625
- out_grad: bfloat16 [16, 2048, 4096], P('pipe', 'ctx'), may hold values from -6 to 6
- log_sum: bfloat16 [16, 32, 2048], P('pipe', None, 'ctx'), may hold values from 2 to 4
- row_delta: bfloat16 [16, 32, 2048], P('pipe', None, 'ctx'), may hold values from -5 to 5
- chosen: int32 [16, 4, 2], P('pipe'), may hold values from 0 to 2, as said below
Outputs:
- query_grads: bfloat16 [16, 2048, 4096], P('pipe', 'ctx')
- key_grads: bfloat16 [16, 2048, 512], P('pipe', 'ctx')
- value_grads: bfloat16 [16, 2048, 512], P('pipe', 'ctx')
- handed_back: bfloat16 [16, 2048, 4096], P('pipe', 'ctx')
The draws below stay inside these ranges and needn't reach their ends.
Inputs may be any that keep to these rules, and one draw needn't show every extreme that they name: Row b of chosen[s] lists distinct key blocks below b first; a row with fewer than 2 earlier blocks is filled with b itself after them; the last row names block 2.
All inputs are finite; a program needn't handle non-finite values.
Results may differ from the reference program's by a relative error of at most 0.0052.
Values may be sent and summed in bfloat16 or wider, within the bound.
A program may use at most 128 MiB of HBM per device.

```python
import jax
import jax.numpy as jnp
from jax import lax

H = 32
KVH = 4
HD = 128
BLOCK = 512
SEL = 2
SEQ = 2048
NB = 4
SECTIONS = 16


def draw_chosen(key, part):
    key = jax.random.fold_in(key, 7)
    row_keys = jax.random.split(key, SECTIONS * NB)
    ranks = jax.vmap(lambda one_key: jax.random.permutation(one_key, NB))(row_keys).reshape(SECTIONS, NB, NB).astype(jnp.int32)
    columns_only = jnp.arange(NB, dtype=jnp.int32)[None, None, :]
    rows_only = jnp.arange(NB, dtype=jnp.int32)[None, :, None]
    forced = (rows_only == NB - 1) & (columns_only == NB - 2)
    ranks = jnp.where(forced, NB + 1, ranks)
    filler = jnp.zeros((SECTIONS, NB, SEL), jnp.int32)
    ranks = jnp.concatenate([ranks, filler], axis=2)
    columns = jnp.arange(NB + SEL, dtype=jnp.int32)[None, None, :]
    rows_here = jnp.arange(NB, dtype=jnp.int32)[None, :, None]
    attention_logits = jnp.where(columns < rows_here, ranks, -1 - columns)
    unused, picked = lax.top_k(attention_logits, SEL)
    picked = picked.astype(jnp.int32)
    picked = jnp.where(picked < rows_here, picked, jnp.broadcast_to(rows_here, picked.shape))
    return picked.astype(jnp.int32)


def steps_of(rng, shape, shards, low, top_value):
    def one(axis_at, shards_of):
        heights = jax.random.uniform(jax.random.fold_in(jax.random.fold_in(rng, 6), axis_at), (shards_of,), jnp.float32, low / len(shards), top_value / len(shards))
        return jnp.repeat(jnp.exp(heights), shape[axis_at] // shards_of).reshape((-1,) + (1,) * (len(shape) - axis_at - 1))

    loudness = one(*shards[0])
    for cut in shards[1:]:
        loudness = loudness * one(*cut)
    return loudness


def centred(rng, dims, scale, reach, shards=(), kind=jnp.bfloat16):
    drawn = scale * jax.random.normal(rng, dims, jnp.float32)
    if shards:
        drawn = drawn * steps_of(rng, dims, shards, -0.22, 0.18)
    return jnp.clip(drawn, -reach, reach).astype(kind)


def setup_inputs(seed: int = 0) -> dict:
    streams_of = jax.random.split(jax.random.key(seed), 8)
    return {
        "queries": centred(streams_of[0], (SECTIONS, SEQ, H * HD), 1.0, 6.0, ((0, 16), (1, 16))),
        "key_heads": centred(streams_of[1], (SECTIONS, SEQ, KVH * HD), 1.0, 6.0, ((0, 16), (1, 16))),
        "value_heads": centred(streams_of[2], (SECTIONS, SEQ, KVH * HD), 0.088, 0.59765625, ((0, 16), (1, 16))),
        "out_grad": centred(streams_of[3], (SECTIONS, SEQ, H * HD), 1.0, 6.0, ((0, 16), (1, 16))),
        "log_sum": jnp.clip(2.0 + 2.0 * jax.random.uniform(streams_of[4], (SECTIONS, H, SEQ), jnp.float32) ** steps_of(streams_of[4], (SECTIONS, H, SEQ), ((0, 16), (2, 16)), -0.2, 0.2), 2.0, 4.0).astype(jnp.bfloat16),
        "row_delta": centred(streams_of[5], (SECTIONS, H, SEQ), 1.0, 5.0, ((0, 16), (2, 16))),
        "chosen": draw_chosen(jax.random.fold_in(streams_of[7], 71), 0),
    }


def round_low(values):
    return lax.optimization_barrier(values.astype(jnp.bfloat16)).astype(jnp.float32)


def section_grads(inputs):
    queries, key_heads, value_heads, out_grad, log_sum, row_delta, chosen = inputs
    groups = H // KVH
    softmax_scale = HD ** -0.5
    query_blocks = queries.reshape(NB, BLOCK, KVH, groups, HD)
    grad_blocks = out_grad.reshape(NB, BLOCK, KVH, groups, HD)
    key_blocks = key_heads.reshape(NB, BLOCK, KVH, HD)
    value_blocks = value_heads.reshape(NB, BLOCK, KVH, HD)
    sum_blocks = log_sum.astype(jnp.float32).reshape(KVH, groups, NB, BLOCK).transpose(2, 0, 1, 3)
    delta_blocks = row_delta.astype(jnp.float32).reshape(KVH, groups, NB, BLOCK).transpose(2, 0, 1, 3)
    causal = jnp.arange(BLOCK)[None, :] <= jnp.arange(BLOCK)[:, None]

    def one_block(carried, block_index):
        key_acc, value_acc = carried
        query_tile = query_blocks[block_index].astype(jnp.float32)
        gradient_tile = grad_blocks[block_index].astype(jnp.float32)
        row_sums = sum_blocks[block_index]
        deltas = delta_blocks[block_index]
        query_gradient_total = jnp.zeros((BLOCK, KVH, groups, HD), jnp.float32)
        for entry_index in range(SEL + 1):
            if entry_index < SEL:
                target = chosen[block_index, entry_index]
                allowed = jnp.broadcast_to(target < block_index, (BLOCK, BLOCK))
            else:
                target = block_index
                allowed = causal
            key_tile = key_blocks[target].astype(jnp.float32)
            value_tile = value_blocks[target].astype(jnp.float32)
            attention_logits = jnp.einsum('oifl,mil->ifom', query_tile, key_tile) * softmax_scale
            attn_probs = jnp.where(allowed, jnp.exp(attention_logits - row_sums[..., None]), 0.0)
            probability_reduced = round_low(attn_probs)
            value_portion = jnp.einsum('imho,himp->oip', probability_reduced, gradient_tile)
            probability_gradient = jnp.einsum('oifl,mil->ifom', gradient_tile, value_tile)
            logit_gradient = round_low(attn_probs * (probability_gradient - deltas[..., None]))
            query_gradient_total = query_gradient_total + jnp.einsum('mtuf,fmw->umtw', logit_gradient, key_tile) * softmax_scale
            key_portion = jnp.einsum('imho,himp->oip', logit_gradient, query_tile) * softmax_scale
            key_acc = key_acc.at[target].add(key_portion)
            value_acc = value_acc.at[target].add(value_portion)
        return (key_acc, value_acc), query_gradient_total

    zero_keys = jnp.zeros((NB, BLOCK, KVH, HD), jnp.float32)
    (key_acc, value_acc), query_all = lax.scan(one_block, (zero_keys, zero_keys), jnp.arange(NB, dtype=jnp.int32))
    query_grads = query_all.reshape(SEQ, H * HD).astype(jnp.bfloat16)
    key_grads = key_acc.reshape(SEQ, KVH * HD).astype(jnp.bfloat16)
    value_grads = value_acc.reshape(SEQ, KVH * HD).astype(jnp.bfloat16)
    return query_grads, key_grads, value_grads


def reference(queries, key_heads, value_heads, out_grad, log_sum, row_delta, chosen):
    query_grads, key_grads, value_grads = lax.map(section_grads, (queries, key_heads, value_heads, out_grad, log_sum, row_delta, chosen))
    handed_back = jnp.concatenate([query_grads[1:], jnp.zeros_like(query_grads[:1])], axis=0)
    return query_grads, key_grads, value_grads, handed_back
```

```python
import jax
import jax.numpy as jnp
from jax import lax
from jax.experimental import pallas as pl
from jax.experimental.pallas import tpu as pltpu
from jax.sharding import PartitionSpec as P

H = 32
KVH = 4
HD = 128
BLOCK = 512
ROWS = 128
PAIR = 2 * ROWS
SLOTS = 6
LEVELS = 8
LOG2E = 1.4426950408889634
SCALE = HD**-0.5
HEADS = 4
NT = (((1,), (1,)), ((), ()))
NN = (((1,), (0,)), ((), ()))
TN = (((0,), (0,)), ((), ()))
MESH = pl.DeviceIdType.MESH
F32 = jnp.float32
BF16 = jnp.bfloat16


def kernel(
    chosen_ref, q_ref, k_ref, v_ref, g_ref, lse_ref, delta_ref,
    dq_ref, dk_ref, dv_ref, hb_ref,
    qa, ga, kv, wr, acc, dqt, stat, stat_in, rs, rr, es, er, dq_out, fin,
    own_sem, x_s, x_r, qx_s, qx_r, up_s, up_r, w_s, w_r, e_s, e_r,
    rd_s, rd_r, er_s, er_r, dq_s, dq_r, hb_s, hb_r, f_s, f_r,
):
    pipe = lax.axis_index("pipe")
    place = lax.axis_index("ctx")
    z = place // 2
    xh = place % 2
    xo = 1 - xh
    partner = (pipe, z * 2 + xo)
    above = (pipe, ((z + 1) % LEVELS) * 2 + xh)
    below = (pipe, ((z + LEVELS - 1) % LEVELS) * 2 + xh)
    before = ((pipe + 15) % 16, place)
    after = ((pipe + 1) % 16, place)
    chain = jnp.where(z <= 5, z, z - 4)
    chain_above = jnp.where(z <= 4, z + 1, jnp.where(z == 7, 0, z - 3))
    wrap = jnp.where(z == 7, 4, jnp.where(z <= 2, 3 - z, 0))
    wrap_below = jnp.where(z <= 3, 4 - z, 0)
    last_block = z >= 6
    second = (chosen_ref[0, 3, 0] + chosen_ref[0, 3, 1]) == 3

    def remote(src, dst, send, recv, device):
        return pltpu.make_async_remote_copy(
            src_ref=src, dst_ref=dst, send_sem=send, recv_sem=recv,
            device_id=device, device_id_type=MESH,
        )

    def lanes(start, size):
        return pl.ds(pl.multiple_of(start, 128), size)

    def rows(start, size):
        return pl.ds(pl.multiple_of(start, 128), size)

    def kv_swap(j, t):
        src = (k_ref, v_ref)[t]
        return remote(
            src.at[0, :, lanes((2 * xo + j) * HD, HD)],
            kv.at[j, 0, t, rows(xh * ROWS, ROWS)],
            x_s.at[j, t], x_r.at[j, t], partner,
        )

    def kv_own(j, t):
        src = (k_ref, v_ref)[t]
        return pltpu.make_async_copy(
            src.at[0, :, lanes((2 * xh + j) * HD, HD)],
            kv.at[j, 0, t, rows(xh * ROWS, ROWS)],
            own_sem.at[j, t],
        )

    def q_swap(j, t):
        src, dst = ((q_ref, qa), (g_ref, ga))[t]
        return remote(
            src.at[0, :, lanes(xo * 2048 + j * 1024, 1024)],
            dst.at[xh, :, pl.ds(j * 1024, 1024)],
            qx_s.at[j, t], qx_r.at[j, t], partner,
        )

    def q_own(j, t):
        src, dst = ((q_ref, qa), (g_ref, ga))[t]
        return pltpu.make_async_copy(
            src.at[0, :, lanes(xh * 2048 + j * 1024, 1024)],
            dst.at[xh, :, pl.ds(j * 1024, 1024)],
            own_sem.at[2 + j, t],
        )

    def stat_swap(t):
        src = (lse_ref, delta_ref)[t]
        return remote(
            src.at[0, pl.ds(pl.multiple_of(xo * 16, 16), 16)],
            stat_in.at[t], x_s.at[2, t], x_r.at[2, t], partner,
        )

    def up(j, d):
        return remote(kv.at[j, d], kv.at[j, d + 1], up_s.at[j, d], up_r.at[j, d + 1], above)

    def up_in(j, d):
        return remote(kv.at[j, d - 1], kv.at[j, d], up_s.at[j, d - 1], up_r.at[j, d], above)

    def round_first(j):
        return remote(kv.at[j, 0], wr.at[j, 0], w_s.at[j, 0], w_r.at[j, 0], below)

    def round_on(j, w):
        return remote(wr.at[j, w - 1], wr.at[j, w], w_s.at[j, w], w_r.at[j, w], below)

    def round_in(j, w):
        return remote(wr.at[j, w], wr.at[j, w], w_s.at[j, w], w_r.at[j, w], below)

    def extra(j, d):
        return remote(kv.at[j, d], kv.at[j, d], e_s.at[j, d - 4], e_r.at[j, d - 4], below)

    def down(j, d):
        return remote(rs.at[j, d], rr.at[j, d - 1], rd_s.at[j, d], rd_r.at[j, d - 1], below)

    def down_in(j, d):
        return remote(rs.at[j, d + 1], rr.at[j, d], rd_s.at[j, d + 1], rd_r.at[j, d], below)

    def extra_back(j, e):
        return remote(es.at[j, e], er.at[j, e], er_s.at[j, e], er_r.at[j, e], above)

    def extra_on(j, e):
        return remote(er.at[j, e], er.at[j, e], er_s.at[j, e], er_r.at[j, e], above)

    def dq_swap(j):
        return remote(
            dq_out.at[j], dq_ref.at[0, :, lanes(xh * 2048 + j * 1024, 1024)],
            dq_s.at[j], dq_r.at[j], partner,
        )

    def dq_in(j):
        return remote(
            dq_out.at[j], dq_ref.at[0, :, lanes(xo * 2048 + j * 1024, 1024)],
            dq_s.at[j], dq_r.at[j], partner,
        )

    def hand_back(j, column):
        part = lanes(column * 2048 + j * 1024, 1024)
        return remote(
            dq_ref.at[0, :, part], hb_ref.at[0, :, part],
            hb_s.at[j, column], hb_r.at[j, column], before,
        )

    def fin_swap(j, t):
        dst = (dk_ref, dv_ref)[t]
        return remote(
            fin.at[j, t, rows(xo * ROWS, ROWS)],
            dst.at[0, :, lanes((2 * xh + j) * HD, HD)],
            f_s.at[j, t], f_r.at[j, t], partner,
        )

    def unit(j, r, d, first, masked=False):
        keys = kv[j, d, 0]
        values = kv[j, d, 1]
        d_keys = None
        d_values = None
        for c in range(8 // HEADS):
            base = j * 1024 + c * HEADS * HD
            head = j * 8 + c * HEADS
            queries = jnp.concatenate(
                [qa[r, :, base + i * HD : base + (i + 1) * HD] for i in range(HEADS)], axis=0
            )
            grads = jnp.concatenate(
                [ga[r, :, base + i * HD : base + (i + 1) * HD] for i in range(HEADS)], axis=0
            )
            lse = jnp.concatenate(
                [stat[0, r, pl.ds(head + i, 1), :] for i in range(HEADS)], axis=1
            )
            delta = jnp.concatenate(
                [stat[1, r, pl.ds(head + i, 1), :] for i in range(HEADS)], axis=1
            )
            scores = lax.dot_general(keys, queries, NT, preferred_element_type=F32)
            probs = jnp.exp2(scores * (SCALE * LOG2E) - lse)
            if masked:
                shape = (PAIR, HEADS * HD)
                key_at = lax.broadcasted_iota(jnp.int32, shape, 0)
                query_at = lax.broadcasted_iota(jnp.int32, shape, 1) % HD + r * ROWS
                probs = jnp.where(key_at <= query_at, probs, 0.0)
            prob_grads = lax.dot_general(values, grads, NT, preferred_element_type=F32)
            score_grads = (probs * (prob_grads - delta)).astype(BF16)
            probs_low = probs.astype(BF16)
            part_v = lax.dot_general(probs_low, grads, NN, preferred_element_type=F32)
            part_k = lax.dot_general(score_grads, queries, NN, preferred_element_type=F32)
            d_values = part_v if d_values is None else d_values + part_v
            d_keys = part_k if d_keys is None else d_keys + part_k
            dqt[r, :, base : base + HEADS * HD] += lax.dot_general(
                keys, score_grads, TN, preferred_element_type=F32
            )
        if first:
            acc[j, d, 0] = d_keys
            acc[j, d, 1] = d_values
        else:
            acc[j, d, 0] += d_keys
            acc[j, d, 1] += d_values

    def has(d):
        return (d <= chain) | (last_block & (d >= 4))

    def gather_step(j, k):
        @pl.when(k <= chain)
        def _():
            up_in(j, k).wait_recv()

        @pl.when(k + 1 <= chain_above)
        def _():
            up(j, k).start()

        @pl.when(k <= wrap)
        def _():
            round_in(j, k - 1).wait_recv()

        @pl.when(k + 1 <= wrap_below)
        def _():
            round_on(j, k).start()

        @pl.when((z == 7) & ((k == 3) | (k == 4)))
        def _():
            kv[j, k + 1] = jnp.where(second, wr[j, k - 1], wr[j, k - 3])
            extra(j, k + 1).start()

        @pl.when((z == 6) & (k >= 4))
        def _():
            extra(j, k).wait_recv()

    def starts_chain(d):
        return d + 1 > chain_above

    def send_down(j, d, ready):
        @pl.when((d <= chain) & starts_chain(d) & ready)
        def _():
            rs[j, d] = acc[j, d].astype(BF16)
            down(j, d).start()

        @pl.when((d <= chain) & jnp.logical_not(starts_chain(d)) & jnp.logical_not(ready))
        def _():
            down_in(j, d).wait_recv()
            rs[j, d] = (acc[j, d] + rr[j, d].astype(F32)).astype(BF16)
            down(j, d).start()

        @pl.when((z == 6) & (d >= 4) & ready)
        def _():
            es[j, d - 4] = acc[j, d].astype(BF16)
            extra_back(j, d - 4).start()

        @pl.when((z == 7) & (d >= 4) & jnp.logical_not(ready))
        def _():
            extra_on(j, d - 4).wait_recv()
            es[j, d - 4] = (acc[j, d] + er[j, d - 4].astype(F32)).astype(BF16)
            extra_back(j, d - 4).start()

    def pass_extra(j, e):
        @pl.when((z <= 2) | ((z == 3) & (e == 1)))
        def _():
            extra_on(j, e).wait_recv()

        @pl.when((z <= 1) | ((z == 2) & (e == 1)))
        def _():
            extra_on(j, e).start()

    def finish_keys(j):
        @pl.when(z <= 6)
        def _():
            down_in(j, 0).wait_recv()
            acc[j, 0] += rr[j, 0].astype(F32)

        @pl.when(z <= 3)
        def _():
            mine = second == (z >= 2)
            acc[j, 0] += jnp.where(mine, er[j, z % 2].astype(F32), 0.0)

        fin[j, 0] = (acc[j, 0, 0] * SCALE).astype(BF16)
        fin[j, 1] = acc[j, 0, 1].astype(BF16)
        for t in range(2):
            fin_swap(j, t).start()
        columns = lanes((2 * xh + j) * HD, HD)
        dk_ref[0, :, columns] = fin[j, 0, rows(xh * ROWS, ROWS)]
        dv_ref[0, :, columns] = fin[j, 1, rows(xh * ROWS, ROWS)]

    def finish_queries(j):
        for i in range(8):
            cols = slice(j * 1024 + i * HD, j * 1024 + (i + 1) * HD)
            dq_out[j, :, i * HD : (i + 1) * HD] = (dqt[xo, :, cols].T * SCALE).astype(BF16)
        dq_swap(j).start()
        for i in range(8):
            cols = slice(j * 1024 + i * HD, j * 1024 + (i + 1) * HD)
            dq_ref[0, :, lanes(xh * 2048 + j * 1024 + i * HD, HD)] = (
                dqt[xh, :, cols].T * SCALE
            ).astype(BF16)

        @pl.when(pipe > 0)
        def _():
            hand_back(j, xh).start()

    def hand_on(j):
        dq_in(j).wait_recv()

        @pl.when(pipe > 0)
        def _():
            hand_back(j, xo).start()

    barrier = pltpu.get_barrier_semaphore()
    for device in (partner, above, below, before, after):
        pl.semaphore_signal(barrier, inc=1, device_id=device, device_id_type=MESH)
    pl.semaphore_wait(barrier, 5)

    for j in range(2):
        for t in range(2):
            kv_swap(j, t).start()
            kv_own(j, t).start()
    for t in range(2):
        stat_swap(t).start()
        for j in range(2):
            q_own(j, t).start()

    dqt[...] = jnp.zeros_like(dqt)
    own_rows = pl.ds(pl.multiple_of(xh * 16, 16), 16)
    stat[0, xh] = lse_ref[0, own_rows].astype(F32) * LOG2E
    stat[1, xh] = delta_ref[0, own_rows].astype(F32)

    @pl.when(pipe == 15)
    def _():
        hb_ref[...] = jnp.zeros_like(hb_ref)

    for j in range(2):
        for t in range(2):
            kv_own(j, t).wait()
            q_own(j, t).wait()

    def first_step(j):
        for t in range(2):
            kv_swap(j, t).wait_recv()

        @pl.when(chain_above >= 1)
        def _():
            up(j, 0).start()

        @pl.when(wrap_below >= 1)
        def _():
            round_first(j).start()

    first_step(0)
    for t in range(2):
        q_swap(0, t).start()
    for t in range(2):
        stat_swap(t).wait_recv()
    stat[0, xo] = stat_in[0].astype(F32) * LOG2E
    stat[1, xo] = stat_in[1].astype(F32)

    unit(0, xh, 0, True, True)

    def phase_a(k, carry):
        gather_step(0, k)

        @pl.when(has(k))
        def _():
            unit(0, xh, k, True)

        return carry

    lax.fori_loop(1, SLOTS, phase_a, 0)
    first_step(1)
    for t in range(2):
        q_swap(0, t).wait_recv()
        q_swap(1, t).start()

    unit(1, xh, 0, True, True)

    def phase_b(k, carry):
        gather_step(1, k)
        far = SLOTS - k

        @pl.when(has(far))
        def _():
            unit(0, xo, far, False)

        send_down(0, far, True)

        @pl.when(has(k))
        def _():
            unit(1, xh, k, True)

        return carry

    lax.fori_loop(1, SLOTS, phase_b, 0)
    unit(0, xo, 0, False, True)
    finish_queries(0)
    for t in range(2):
        q_swap(1, t).wait_recv()

    def phase_c(k, carry):
        far = SLOTS - k

        @pl.when(has(far))
        def _():
            unit(1, xo, far, False)

        send_down(1, far, True)
        send_down(0, far, False)
        return carry

    lax.fori_loop(1, SLOTS, phase_c, 0)
    unit(1, xo, 0, False, True)
    finish_queries(1)
    hand_on(0)
    for e in range(2):
        pass_extra(0, e)
    finish_keys(0)

    def phase_d(k, carry):
        send_down(1, SLOTS - k, False)
        return carry

    lax.fori_loop(1, SLOTS, phase_d, 0)
    hand_on(1)
    for e in range(2):
        pass_extra(1, e)
    finish_keys(1)

    for j in range(2):
        for t in range(2):
            fin_swap(j, t).wait_recv()
            fin_swap(j, t).wait_send()
            kv_swap(j, t).wait_send()
            q_swap(j, t).wait_send()
        dq_swap(j).wait_send()

        @pl.when(pipe > 0)
        def _():
            for column in range(2):
                hand_back(j, column).wait_send()

        @pl.when(pipe < 15)
        def _():
            for column in range(2):
                hand_back(j, column).wait_recv()

        for d in range(SLOTS):
            @pl.when(d + 1 <= chain_above)
            def _():
                up(j, d).wait_send()

            if d >= 1:
                @pl.when(d <= chain)
                def _():
                    down(j, d).wait_send()

            if d >= 4:
                @pl.when(z == 7)
                def _():
                    extra(j, d).wait_send()

        for w in range(4):
            @pl.when(w + 1 <= wrap_below)
            def _():
                round_on(j, max(w, 1)).wait_send() if w else round_first(j).wait_send()

        for e in range(2):
            @pl.when(last_block)
            def _():
                extra_back(j, e).wait_send()

            @pl.when((z <= 1) | ((z == 2) & (e == 1)))
            def _():
                extra_on(j, e).wait_send()
    for t in range(2):
        stat_swap(t).wait_send()


def per_device(queries, key_heads, value_heads, out_grad, log_sum, row_delta, chosen):
    vmem = pl.BlockSpec(memory_space=pltpu.VMEM)
    dma = pltpu.SemaphoreType.DMA
    level = (2, PAIR, HD)
    flops = 5 * 2 * ROWS * H * HD * 1536
    return pl.pallas_call(
        kernel,
        out_shape=(
            jax.ShapeDtypeStruct(queries.shape, BF16),
            jax.ShapeDtypeStruct(key_heads.shape, BF16),
            jax.ShapeDtypeStruct(value_heads.shape, BF16),
            jax.ShapeDtypeStruct(queries.shape, BF16),
        ),
        in_specs=[pl.BlockSpec(memory_space=pltpu.SMEM)] + [vmem] * 6,
        out_specs=(vmem,) * 4,
        scratch_shapes=[
            pltpu.VMEM((2, ROWS, 2048), BF16),
            pltpu.VMEM((2, ROWS, 2048), BF16),
            pltpu.VMEM((2, SLOTS) + level, BF16),
            pltpu.VMEM((2, 4) + level, BF16),
            pltpu.VMEM((2, SLOTS) + level, F32),
            pltpu.VMEM((2, HD, 2048), F32),
            pltpu.VMEM((2, 2, 16, ROWS), F32),
            pltpu.VMEM((2, 16, ROWS), BF16),
            pltpu.VMEM((2, SLOTS) + level, BF16),
            pltpu.VMEM((2, SLOTS) + level, BF16),
            pltpu.VMEM((2, 2) + level, BF16),
            pltpu.VMEM((2, 2) + level, BF16),
            pltpu.VMEM((2, ROWS, 1024), BF16),
            pltpu.VMEM((2,) + level, BF16),
            dma((4, 2)),
            dma((3, 2)), dma((3, 2)),
            dma((2, 2)), dma((2, 2)),
            dma((2, SLOTS)), dma((2, SLOTS)),
            dma((2, 4)), dma((2, 4)),
            dma((2, 2)), dma((2, 2)),
            dma((2, SLOTS)), dma((2, SLOTS)),
            dma((2, 2)), dma((2, 2)),
            dma((2,)), dma((2,)),
            dma((2, 2)), dma((2, 2)),
            dma((2, 2)), dma((2, 2)),
        ],
        compiler_params=pltpu.CompilerParams(
            collective_id=0, has_side_effects=True, vmem_limit_bytes=40 * 2**20
        ),
        cost_estimate=pl.CostEstimate(
            flops=flops, bytes_accessed=6 * 2**20, transcendentals=ROWS * H * 1536
        ),
        name="block_attention_backward",
    )(chosen, queries, key_heads, value_heads, out_grad, log_sum, row_delta)


def solution(mesh):
    heads = P("pipe", "ctx", None)
    stats = P("pipe", None, "ctx")
    return jax.shard_map(
        per_device,
        mesh=mesh,
        in_specs=(heads, heads, heads, heads, stats, stats, P("pipe", None, None)),
        out_specs=(heads, heads, heads, heads),
        check_vma=False,
    )
```

```python
import jax
import jax.numpy as jnp
from jax import lax
from jax.experimental import pallas as pl
from jax.experimental.pallas import tpu as pltpu
from jax.sharding import PartitionSpec as P

H = 32
KVH = 4
HD = 128
BLOCK = 512
ROWS = 128
PAIR = 2 * ROWS
SLOTS = 6
LEVELS = 8
LOG2E = 1.4426950408889634
SCALE = HD**-0.5
HEADS = 4
NT = (((1,), (1,)), ((), ()))
NN = (((1,), (0,)), ((), ()))
TN = (((0,), (0,)), ((), ()))
MESH = pl.DeviceIdType.MESH
F32 = jnp.float32
BF16 = jnp.bfloat16


def kernel(
    chosen_ref, q_ref, k_ref, v_ref, g_ref, lse_ref, delta_ref,
    dq_ref, dk_ref, dv_ref, hb_ref,
    qa, ga, kv, wr, acc, dqt, stat, stat_in, rs, rr, rs_wide, rr_wide, es, er, dq_out, fin,
    own_sem, x_s, x_r, qx_s, qx_r, up_s, up_r, w_s, w_r, e_s, e_r,
    rd_s, rd_r, er_s, er_r, dq_s, dq_r, hb_s, hb_r, f_s, f_r,
):
    pipe = lax.axis_index("pipe")
    place = lax.axis_index("ctx")
    z = place // 2
    xh = place % 2
    xo = 1 - xh

    def level(number):
        return (pipe, number * 2 + xh)

    partner = (pipe, z * 2 + xo)
    above = level((z + 1) % LEVELS)
    below = level((z + LEVELS - 1) % LEVELS)
    before = ((pipe + 15) % 16, place)
    after = ((pipe + 1) % 16, place)
    chain = jnp.where(z <= 5, z, z - 4)
    chain_above = jnp.where(z <= 4, z + 1, jnp.where(z == 7, 0, z - 3))
    last_block = z >= 6
    second = (chosen_ref[0, 0, 3] + chosen_ref[0, 1, 3]) == 3

    def remote(src, dst, send, recv, device):
        return pltpu.make_async_remote_copy(
            src_ref=src, dst_ref=dst, send_sem=send, recv_sem=recv,
            device_id=device, device_id_type=MESH,
        )

    def lanes(start, size):
        return pl.ds(pl.multiple_of(start, 128), size)

    def rows(start, size):
        return pl.ds(pl.multiple_of(start, 128), size)

    def kv_swap(j, t):
        src = (k_ref, v_ref)[t]
        return remote(
            src.at[0, :, lanes((2 * xo + j) * HD, HD)],
            kv.at[j, 0, t, rows(xh * ROWS, ROWS)],
            x_s.at[j, t], x_r.at[j, t], partner,
        )

    def kv_own(j, t):
        src = (k_ref, v_ref)[t]
        return pltpu.make_async_copy(
            src.at[0, :, lanes((2 * xh + j) * HD, HD)],
            kv.at[j, 0, t, rows(xh * ROWS, ROWS)],
            own_sem.at[j, t],
        )

    def q_swap(j, t):
        src, dst = ((q_ref, qa), (g_ref, ga))[t]
        return remote(
            src.at[0, :, lanes(xo * 2048 + j * 1024, 1024)],
            dst.at[xh, :, pl.ds(j * 1024, 1024)],
            qx_s.at[j, t], qx_r.at[j, t], partner,
        )

    def q_own(j, t):
        src, dst = ((q_ref, qa), (g_ref, ga))[t]
        return pltpu.make_async_copy(
            src.at[0, :, lanes(xh * 2048 + j * 1024, 1024)],
            dst.at[xh, :, pl.ds(j * 1024, 1024)],
            own_sem.at[2 + j, t],
        )

    def stat_swap(t):
        src = (lse_ref, delta_ref)[t]
        return remote(
            src.at[0, pl.ds(pl.multiple_of(xo * 16, 16), 16)],
            stat_in.at[0, t], x_s.at[2, t], x_r.at[2, t], partner,
        )

    def stat_own(t):
        src = (lse_ref, delta_ref)[t]
        return pltpu.make_async_copy(
            src.at[0, pl.ds(pl.multiple_of(xh * 16, 16), 16)],
            stat_in.at[1, t], own_sem.at[4, t],
        )

    def up(j, d, t):
        return remote(
            kv.at[j, d, t], kv.at[j, d + 1, t], up_s.at[j, d, t], up_r.at[j, d + 1, t], above
        )

    def up_in(j, d, t):
        return remote(
            kv.at[j, d - 1, t], kv.at[j, d, t], up_s.at[j, d - 1, t], up_r.at[j, d, t], above
        )

    def round_first(j, t):
        return remote(
            kv.at[j, 0, t], wr.at[j, z, t], w_s.at[j, 0, t], w_r.at[j, z, t],
            level(jnp.where(z == 3, 1, 7)),
        )

    def round_on(j, t):
        return remote(
            wr.at[j, 3, t], wr.at[j, 3, t], w_s.at[j, 1, t], w_r.at[j, 3, t], level(7)
        )

    def round_in(j, source, t):
        return remote(
            wr.at[j, source, t], wr.at[j, source, t], w_s.at[j, 0, t], w_r.at[j, source, t],
            level(7),
        )

    def extra(j, e, t):
        return remote(
            kv.at[j, 4 + e, t], kv.at[j, 4 + e, t], e_s.at[j, e, t], e_r.at[j, e, t], below
        )

    def down(j, d, t):
        return remote(
            rs.at[j, d, t], rr.at[j, d - 1, t], rd_s.at[j, d, t], rd_r.at[j, d - 1, t], below
        )

    def down_wide(j, d, t):
        return remote(
            rs_wide.at[j, d - 1, t], rr_wide.at[j, d - 1, t],
            rd_s.at[j, d, t], rd_r.at[j, d - 1, t], below,
        )

    def down_in(j, d, t):
        return remote(
            rr.at[j, d, t], rr.at[j, d, t], rd_s.at[j, d + 1, t], rd_r.at[j, d, t], below
        )

    def down_wide_in(j, d, t):
        return remote(
            rr_wide.at[j, d, t], rr_wide.at[j, d, t],
            rd_s.at[j, d + 1, t], rd_r.at[j, d, t], below,
        )

    def extra_back(j, e, t, target, way):
        return remote(es.at[j, e, t], er.at[j, e, t], er_s.at[j, way, t], er_r.at[j, e, t], target)

    def extra_on(j, t):
        return remote(er.at[j, 1, t], er.at[j, 1, t], er_s.at[j, 1, t], er_r.at[j, 1, t], level(3))

    def extra_in(j, e, t):
        return remote(er.at[j, e, t], er.at[j, e, t], er_s.at[j, e, t], er_r.at[j, e, t], above)

    def dq_swap(j):
        return remote(
            dq_out.at[j], dq_ref.at[0, :, lanes(xh * 2048 + j * 1024, 1024)],
            dq_s.at[j], dq_r.at[j], partner,
        )

    def dq_in(j):
        return remote(
            dq_out.at[j], dq_ref.at[0, :, lanes(xo * 2048 + j * 1024, 1024)],
            dq_s.at[j], dq_r.at[j], partner,
        )

    def hand_back(j, column):
        part = lanes(column * 2048 + j * 1024, 1024)
        return remote(
            dq_ref.at[0, :, part], hb_ref.at[0, :, part],
            hb_s.at[j, column], hb_r.at[j, column], before,
        )

    def fin_swap(j, t):
        dst = (dk_ref, dv_ref)[t]
        return remote(
            fin.at[j, t, rows(xo * ROWS, ROWS)],
            dst.at[0, :, lanes((2 * xh + j) * HD, HD)],
            f_s.at[j, t], f_r.at[j, t], partner,
        )

    def unit(j, r, d, first, masked=False):
        keys = kv[j, d, 0]
        values = kv[j, d, 1]
        d_keys = None
        d_values = None
        for c in range(8 // HEADS):
            base = j * 1024 + c * HEADS * HD
            head = j * 8 + c * HEADS
            queries = jnp.concatenate(
                [qa[r, :, base + i * HD : base + (i + 1) * HD] for i in range(HEADS)], axis=0
            )
            grads = jnp.concatenate(
                [ga[r, :, base + i * HD : base + (i + 1) * HD] for i in range(HEADS)], axis=0
            )
            lse = jnp.concatenate(
                [stat[0, r, pl.ds(head + i, 1), :] for i in range(HEADS)], axis=1
            )
            delta = jnp.concatenate(
                [stat[1, r, pl.ds(head + i, 1), :] for i in range(HEADS)], axis=1
            )
            scores = lax.dot_general(keys, queries, NT, preferred_element_type=F32)
            probs = jnp.exp2(scores * (SCALE * LOG2E) - lse)
            if masked:
                shape = (PAIR, HEADS * HD)
                key_at = lax.broadcasted_iota(jnp.int32, shape, 0)
                query_at = lax.broadcasted_iota(jnp.int32, shape, 1) % HD + r * ROWS
                probs = jnp.where(key_at <= query_at, probs, 0.0)
            prob_grads = lax.dot_general(values, grads, NT, preferred_element_type=F32)
            score_grads = (probs * (prob_grads - delta)).astype(BF16)
            probs_low = probs.astype(BF16)
            part_v = lax.dot_general(probs_low, grads, NN, preferred_element_type=F32)
            part_k = lax.dot_general(score_grads, queries, NN, preferred_element_type=F32)
            d_values = part_v if d_values is None else d_values + part_v
            d_keys = part_k if d_keys is None else d_keys + part_k
            dqt[r, :, base : base + HEADS * HD] += lax.dot_general(
                keys, score_grads, TN, preferred_element_type=F32
            )
        if first:
            acc[j, d, 0] = d_keys
            acc[j, d, 1] = d_values
        else:
            acc[j, d, 0] += d_keys
            acc[j, d, 1] += d_values

    def has(d):
        return (d <= chain) | (last_block & (d >= 4))

    def arrival(t):
        low = jnp.where((t > z) & (t <= 2 * z), 2 * z + 1 - t, 0)
        five = jnp.where(t == 6, 1, jnp.where(t > 6, 12 - t, 0))
        six = jnp.where(t == 3, 1, jnp.where(t == 7, 2, 0))
        seven = jnp.where(t == 3, 1, jnp.where(t == 4, 2, jnp.where(t == 8, 3, 0)))
        return jnp.where(
            z <= 4, low, jnp.where(z == 5, five, jnp.where(z == 6, six, seven))
        )

    def take(j, d):
        for t in range(2):
            up_in(j, d, t).wait_recv()

            @pl.when(d + 1 <= chain_above)
            def _():
                up(j, d, t).start()

    def choose(j, e):
        kv[j, 4 + e] = jnp.where(second, wr[j, 2 + e], wr[j, e])
        for t in range(2):
            extra(j, e, t).start()

    def extra_levels(j, k):
        @pl.when((z == 1) & (k == 2))
        def _():
            for t in range(2):
                round_in(j, 3, t).wait_recv()
                round_on(j, t).start()

        for e in range(2):
            @pl.when((z == 7) & (k == 3 + e))
            def _():
                for t in range(2):
                    round_in(j, e, t).wait_recv()
                    round_in(j, 2 + e, t).wait_recv()
                choose(j, e)

            @pl.when((z == 6) & (k == 4 + e))
            def _():
                for t in range(2):
                    extra(j, e, t).wait_recv()

    def gather(t):
        @pl.when(t <= chain)
        def _():
            take(0, t)

        slot = arrival(t)

        @pl.when(slot >= 1)
        def _():
            take(1, slot)

        at = jnp.where(z <= 3, jnp.maximum(2 * z, 1), jnp.where(z == 4, 4, 2))

        @pl.when((t == at) & (chain_above >= 1))
        def _():
            for kind in range(2):
                up(1, 0, kind).start()

        @pl.when((t == 3) & (z <= 3))
        def _():
            for kind in range(2):
                round_first(1, kind).start()

        extra_levels(0, t)
        extra_levels(1, t - 4)

    def starts_chain(d):
        return d + 1 > chain_above

    def send_first(j, d):
        @pl.when((d <= chain) & starts_chain(d))
        def _():
            for t in range(2):
                rs[j, d, t] = acc[j, d, t].astype(BF16)
                down(j, d, t).start()

        @pl.when((z == 6) & (d >= 4))
        def _():
            for t in range(2):
                es[j, d - 4, t] = acc[j, d, t].astype(BF16)
                extra_back(j, d - 4, t, above, d - 4).start()

    def send_on(j, d):
        due = (d >= 1) & (d <= chain) & jnp.logical_not(starts_chain(d))

        @pl.when(due & (z >= 3))
        def _():
            for t in range(2):
                down_in(j, d, t).wait_recv()
                rs[j, d, t] = (acc[j, d, t] + rr[j, d, t].astype(F32)).astype(BF16)
                down(j, d, t).start()

        @pl.when(due & (z == 2))
        def _():
            for t in range(2):
                down_in(j, d, t).wait_recv()
                rs_wide[j, d - 1, t] = acc[j, d, t] + rr[j, d, t].astype(F32)
                down_wide(j, d, t).start()

        @pl.when(due & (z == 1))
        def _():
            for t in range(2):
                down_wide_in(j, d, t).wait_recv()
                rs_wide[j, d - 1, t] = acc[j, d, t] + rr_wide[j, d, t]
                down_wide(j, d, t).start()

    def extra_sum(j, e):
        @pl.when(z == 7)
        def _():
            for t in range(2):
                extra_in(j, e, t).wait_recv()
                es[j, e, t] = (acc[j, 4 + e, t] + er[j, e, t].astype(F32)).astype(BF16)
                if e == 0:
                    extra_back(j, 0, t, level(0), 0).start()
                    extra_back(j, 0, t, level(2), 2).start()
                else:
                    extra_back(j, 1, t, level(1), 1).start()

    def extra_relay(j):
        @pl.when(z == 1)
        def _():
            for t in range(2):
                extra_in(j, 1, t).wait_recv()
                extra_on(j, t).start()

    def finish_keys(j):
        @pl.when(z <= 3)
        def _():
            e = z % 2

            @pl.when(z != 1)
            def _():
                for t in range(2):
                    extra_in(j, e, t).wait_recv()

            mine = second == (z >= 2)
            acc[j, 0] += jnp.where(mine, er[j, e].astype(F32), 0.0)

        for t in range(2):
            @pl.when((z >= 2) & (z <= 6))
            def _():
                down_in(j, 0, t).wait_recv()
                acc[j, 0, t] += rr[j, 0, t].astype(F32)

            @pl.when(z <= 1)
            def _():
                down_wide_in(j, 0, t).wait_recv()
                acc[j, 0, t] += rr_wide[j, 0, t]

            fin[j, t] = (acc[j, 0, t] * (SCALE if t == 0 else 1.0)).astype(BF16)
            fin_swap(j, t).start()
        columns = lanes((2 * xh + j) * HD, HD)
        dk_ref[0, :, columns] = fin[j, 0, rows(xh * ROWS, ROWS)]
        dv_ref[0, :, columns] = fin[j, 1, rows(xh * ROWS, ROWS)]

    def finish_queries(j):
        for i in range(8):
            cols = slice(j * 1024 + i * HD, j * 1024 + (i + 1) * HD)
            dq_out[j, :, i * HD : (i + 1) * HD] = (dqt[xo, :, cols].T * SCALE).astype(BF16)
        dq_swap(j).start()
        for i in range(8):
            cols = slice(j * 1024 + i * HD, j * 1024 + (i + 1) * HD)
            dq_ref[0, :, lanes(xh * 2048 + j * 1024 + i * HD, HD)] = (
                dqt[xh, :, cols].T * SCALE
            ).astype(BF16)

        @pl.when(pipe > 0)
        def _():
            hand_back(j, xh).start()

    def hand_on(j):
        dq_in(j).wait_recv()

        @pl.when(pipe > 0)
        def _():
            hand_back(j, xo).start()

    for j in range(2):
        for t in range(2):
            kv_own(j, t).start()
    for t in range(2):
        stat_own(t).start()
        for j in range(2):
            q_own(j, t).start()

    barrier = pltpu.get_barrier_semaphore()

    def greet(device):
        pl.semaphore_signal(barrier, inc=1, device_id=device, device_id_type=MESH)

    for device in (partner, above, below, before, after):
        greet(device)

    @pl.when((z == 1) | (z == 2))
    def _():
        greet(level(7))

    @pl.when(z == 7)
    def _():
        greet(level(1))
        greet(level(2))

    @pl.when(z == 1)
    def _():
        greet(level(3))

    @pl.when(z == 3)
    def _():
        greet(level(1))

    far_greetings = jnp.where((z == 1) | (z == 7), 2, jnp.where((z == 2) | (z == 3), 1, 0))
    pl.semaphore_wait(barrier, 5 + far_greetings)

    for j in range(2):
        for t in range(2):
            kv_swap(j, t).start()
        if j == 0:
            for t in range(2):
                stat_swap(t).start()

    dqt[...] = jnp.zeros_like(dqt)

    @pl.when(pipe == 15)
    def _():
        hb_ref[...] = jnp.zeros_like(hb_ref)

    for t in range(2):
        stat_own(t).wait()
    stat[0, xh] = stat_in[1, 0].astype(F32) * LOG2E
    stat[1, xh] = stat_in[1, 1].astype(F32)
    for j in range(2):
        for t in range(2):
            kv_own(j, t).wait()
            q_own(j, t).wait()

    for t in range(2):
        kv_swap(0, t).wait_recv()

        @pl.when(chain_above >= 1)
        def _():
            up(0, 0, t).start()

        @pl.when(z <= 3)
        def _():
            round_first(0, t).start()

    for j in range(2):
        for t in range(2):
            q_swap(j, t).start()
    for t in range(2):
        kv_swap(1, t).wait_recv()
        stat_swap(t).wait_recv()
    stat[0, xo] = stat_in[0, 0].astype(F32) * LOG2E
    stat[1, xo] = stat_in[0, 1].astype(F32)

    unit(0, xh, 0, True, True)

    def phase_a(k, carry):
        gather(k)

        @pl.when(has(k))
        def _():
            unit(0, xh, k, True)

        return carry

    lax.fori_loop(1, SLOTS, phase_a, 0)
    for t in range(2):
        q_swap(0, t).wait_recv()

    def arrived(k):
        return jnp.where(
            last_block, k, jnp.where(z == 5, jnp.where(k == 1, 1, 7 - k), chain + 1 - k)
        )

    def own_rows(k):
        d = arrived(k)

        @pl.when((d >= 1) & has(d))
        def _():
            unit(1, xh, d, True)

    def partner_rows(j, d):
        @pl.when((d >= 1) & has(d))
        def _():
            unit(j, xo, d, False)
            send_first(j, d)

    unit(1, xh, 0, True, True)

    def phase_b(k, carry):
        gather(k + 5)

        def one(n, inner):
            partner_rows(0, 7 - 2 * k - n)
            return inner

        lax.fori_loop(0, 2, one, 0)
        own_rows(k)
        return carry

    lax.fori_loop(1, 3, phase_b, 0)
    gather(8)
    partner_rows(0, 1)
    unit(0, xo, 0, False, True)
    finish_queries(0)
    own_rows(3)
    for e in (1, 0):
        extra_sum(0, e)
    send_on(0, 4)
    for t in range(2):
        q_swap(1, t).wait_recv()

    def phase_c(k, carry):
        gather(k + 5)
        own_rows(k)
        partner_rows(1, arrived(k - 2))
        send_on(0, 7 - k)
        return carry

    lax.fori_loop(4, 6, phase_c, 0)
    hand_on(0)

    def phase_d(n, carry):
        partner_rows(1, arrived(jnp.where(n == 2, 1, 4 + n)))

        @pl.when(n == 0)
        def _():
            send_on(0, 1)

        return carry

    lax.fori_loop(0, 3, phase_d, 0)
    extra_relay(0)
    unit(1, xo, 0, False, True)
    finish_queries(1)
    for e in range(2):
        extra_sum(1, e)

    def phase_e(k, carry):
        send_on(1, SLOTS - k)
        return carry

    extra_relay(1)
    lax.fori_loop(1, 3, phase_e, 0)
    finish_keys(0)
    hand_on(1)
    lax.fori_loop(3, SLOTS, phase_e, 0)
    finish_keys(1)

    for j in range(2):
        for t in range(2):
            fin_swap(j, t).wait_recv()
            fin_swap(j, t).wait_send()
            kv_swap(j, t).wait_send()
            q_swap(j, t).wait_send()
        dq_swap(j).wait_send()

        @pl.when(pipe > 0)
        def _():
            for column in range(2):
                hand_back(j, column).wait_send()

        @pl.when(pipe < 15)
        def _():
            for column in range(2):
                hand_back(j, column).wait_recv()

        for t in range(2):
            for d in range(SLOTS):
                @pl.when(d + 1 <= chain_above)
                def _():
                    up(j, d, t).wait_send()

                if d >= 1:
                    @pl.when((d <= chain) & (z >= 3))
                    def _():
                        down(j, d, t).wait_send()

                if d == 1 or d == 2:
                    @pl.when((d <= chain) & (z <= 2))
                    def _():
                        down_wide(j, d, t).wait_send()

            @pl.when(z <= 3)
            def _():
                round_first(j, t).wait_send()

            @pl.when(z == 1)
            def _():
                round_on(j, t).wait_send()
                extra_on(j, t).wait_send()

            for e in range(2):
                @pl.when(z == 7)
                def _():
                    extra(j, e, t).wait_send()

                @pl.when(last_block)
                def _():
                    extra_back(j, e, t, above, e).wait_send()

            @pl.when(z == 7)
            def _():
                extra_back(j, 0, t, level(2), 2).wait_send()

    for t in range(2):
        stat_swap(t).wait_send()


def write_out(*refs):
    done = refs[12]

    def piece(stage, i, c):
        part = pl.ds(c * 32, 32)
        return pltpu.make_async_copy(
            refs[(i, 8 + i)[stage]].at[0, part], refs[(8 + i, 4 + i)[stage]].at[0, part],
            done.at[stage, i, c],
        )

    pieces = [(i, c) for i in (0, 3, 1, 2) for c in range(4)]
    for i, c in pieces:
        piece(0, i, c).start()
    for i, c in pieces:
        piece(0, i, c).wait()
        piece(1, i, c).start()
    for i, c in pieces:
        piece(1, i, c).wait()


def per_device(queries, key_heads, value_heads, out_grad, log_sum, row_delta, chosen):
    vmem = pl.BlockSpec(memory_space=pltpu.VMEM)
    hbm = pl.BlockSpec(memory_space=pltpu.HBM)
    dma = pltpu.SemaphoreType.DMA
    level = (2, PAIR, HD)
    flops = 5 * 2 * ROWS * H * HD * 1536
    grads = pl.pallas_call(
        kernel,
        out_shape=(
            jax.ShapeDtypeStruct(queries.shape, BF16),
            jax.ShapeDtypeStruct(key_heads.shape, BF16),
            jax.ShapeDtypeStruct(value_heads.shape, BF16),
            jax.ShapeDtypeStruct(queries.shape, BF16),
        ),
        in_specs=[pl.BlockSpec(memory_space=pltpu.SMEM)] + [hbm] * 6,
        out_specs=(vmem,) * 4,
        scratch_shapes=[
            pltpu.VMEM((2, ROWS, 2048), BF16),
            pltpu.VMEM((2, ROWS, 2048), BF16),
            pltpu.VMEM((2, SLOTS) + level, BF16),
            pltpu.VMEM((2, 4) + level, BF16),
            pltpu.VMEM((2, SLOTS) + level, F32),
            pltpu.VMEM((2, HD, 2048), F32),
            pltpu.VMEM((2, 2, 16, ROWS), F32),
            pltpu.VMEM((2, 2, 16, ROWS), BF16),
            pltpu.VMEM((2, SLOTS) + level, BF16),
            pltpu.VMEM((2, SLOTS) + level, BF16),
            pltpu.VMEM((2, 2) + level, F32),
            pltpu.VMEM((2, 2) + level, F32),
            pltpu.VMEM((2, 2) + level, BF16),
            pltpu.VMEM((2, 2) + level, BF16),
            pltpu.VMEM((2, ROWS, 1024), BF16),
            pltpu.VMEM((2,) + level, BF16),
            dma((5, 2)),
            dma((3, 2)), dma((3, 2)),
            dma((2, 2)), dma((2, 2)),
            dma((2, SLOTS, 2)), dma((2, SLOTS, 2)),
            dma((2, 2, 2)), dma((2, 4, 2)),
            dma((2, 2, 2)), dma((2, 2, 2)),
            dma((2, SLOTS, 2)), dma((2, SLOTS, 2)),
            dma((2, 3, 2)), dma((2, 2, 2)),
            dma((2,)), dma((2,)),
            dma((2, 2)), dma((2, 2)),
            dma((2, 2)), dma((2, 2)),
        ],
        compiler_params=pltpu.CompilerParams(
            collective_id=0, has_side_effects=True, vmem_limit_bytes=63 * 2**20
        ),
        cost_estimate=pl.CostEstimate(
            flops=flops, bytes_accessed=6 * 2**20, transcendentals=ROWS * H * 1536
        ),
        name="block_attention_backward",
    )(chosen.transpose(0, 2, 1), queries, key_heads, value_heads, out_grad, log_sum, row_delta)
    anywhere = pl.BlockSpec(memory_space=pl.ANY)
    return pl.pallas_call(
        write_out,
        out_shape=tuple(jax.ShapeDtypeStruct(part.shape, part.dtype) for part in grads),
        in_specs=[anywhere] * 4,
        out_specs=(anywhere,) * 4,
        scratch_shapes=[pltpu.VMEM(part.shape, part.dtype) for part in grads] + [dma((2, 4, 4))],
        name="write_out",
    )(*grads)


def solution(mesh):
    heads = P("pipe", "ctx", None)
    stats = P("pipe", None, "ctx")
    return jax.shard_map(
        per_device,
        mesh=mesh,
        in_specs=(heads, heads, heads, heads, stats, stats, P("pipe", None, None)),
        out_specs=(heads, heads, heads, heads),
        check_vma=False,
    )
```

```python
import jax
import jax.numpy as jnp
from jax import lax
from jax.experimental import pallas as pl
from jax.experimental.pallas import tpu as pltpu
from jax.sharding import PartitionSpec as P

H = 32
KVH = 4
HD = 128
BLOCK = 512
ROWS = 128
PAIR = 2 * ROWS
SLOTS = 6
LEVELS = 8
LOG2E = 1.4426950408889634
SCALE = HD**-0.5
HEADS = 8
NT = (((1,), (1,)), ((), ()))
NN = (((1,), (0,)), ((), ()))
TN = (((0,), (0,)), ((), ()))
MESH = pl.DeviceIdType.MESH
F32 = jnp.float32
BF16 = jnp.bfloat16


def kernel(
    chosen_ref, q_ref, k_ref, v_ref, g_ref, lse_ref, delta_ref,
    dq_ref, dk_ref, dv_ref, hb_ref,
    qa, ga, kv, wr, acc, dqt, stat, stat_in, rs, rr, rs_wide, rr_wide, es, er, dq_out, fin,
    own_sem, x_s, x_r, qx_s, qx_r, up_s, up_r, w_s, w_r, e_s, e_r,
    rd_s, rd_r, er_s, er_r, dq_s, dq_r, hb_s, hb_r, f_s, f_r,
):
    pipe = lax.axis_index("pipe")
    place = lax.axis_index("ctx")
    z = place // 2
    xh = place % 2
    xo = 1 - xh

    def level(number):
        return (pipe, number * 2 + xh)

    partner = (pipe, z * 2 + xo)
    above = level((z + 1) % LEVELS)
    below = level((z + LEVELS - 1) % LEVELS)
    before = ((pipe + 15) % 16, place)
    after = ((pipe + 1) % 16, place)
    chain = jnp.where(z <= 5, z, z - 4)
    chain_above = jnp.where(z <= 4, z + 1, jnp.where(z == 7, 0, z - 3))
    last_block = z >= 6
    second = (chosen_ref[0, 0, 3] + chosen_ref[0, 1, 3]) == 3

    def remote(src, dst, send, recv, device):
        return pltpu.make_async_remote_copy(
            src_ref=src, dst_ref=dst, send_sem=send, recv_sem=recv,
            device_id=device, device_id_type=MESH,
        )

    def lanes(start, size):
        return pl.ds(pl.multiple_of(start, 128), size)

    def rows(start, size):
        return pl.ds(pl.multiple_of(start, 128), size)

    def kv_swap(j, t):
        src = (k_ref, v_ref)[t]
        return remote(
            src.at[0, :, lanes((2 * xo + j) * HD, HD)],
            kv.at[j, 0, t, rows(xh * ROWS, ROWS)],
            x_s.at[j, t], x_r.at[j, t], partner,
        )

    def kv_own(j, t):
        src = (k_ref, v_ref)[t]
        return pltpu.make_async_copy(
            src.at[0, :, lanes((2 * xh + j) * HD, HD)],
            kv.at[j, 0, t, rows(xh * ROWS, ROWS)],
            own_sem.at[j, t],
        )

    def q_swap(j, t):
        src, dst = ((q_ref, qa), (g_ref, ga))[t]
        return remote(
            src.at[0, :, lanes(xo * 2048 + j * 1024, 1024)],
            dst.at[xh, :, pl.ds(j * 1024, 1024)],
            qx_s.at[j, t], qx_r.at[j, t], partner,
        )

    def q_own(j, t):
        src, dst = ((q_ref, qa), (g_ref, ga))[t]
        return pltpu.make_async_copy(
            src.at[0, :, lanes(xh * 2048 + j * 1024, 1024)],
            dst.at[xh, :, pl.ds(j * 1024, 1024)],
            own_sem.at[2 + j, t],
        )

    def stat_swap(t):
        src = (lse_ref, delta_ref)[t]
        return remote(
            src.at[0, pl.ds(pl.multiple_of(xo * 16, 16), 16)],
            stat_in.at[0, t], x_s.at[2, t], x_r.at[2, t], partner,
        )

    def stat_own(t):
        src = (lse_ref, delta_ref)[t]
        return pltpu.make_async_copy(
            src.at[0, pl.ds(pl.multiple_of(xh * 16, 16), 16)],
            stat_in.at[1, t], own_sem.at[4, t],
        )

    def up(j, d, t):
        return remote(
            kv.at[j, d, t], kv.at[j, d + 1, t], up_s.at[j, d, t], up_r.at[j, d + 1, t], above
        )

    def up_in(j, d, t):
        return remote(
            kv.at[j, d - 1, t], kv.at[j, d, t], up_s.at[j, d - 1, t], up_r.at[j, d, t], above
        )

    def round_first(j, t):
        return remote(
            kv.at[j, 0, t], wr.at[j, z, t], w_s.at[j, 0, t], w_r.at[j, z, t],
            level(jnp.where(z == 3, 1, 7)),
        )

    def round_on(j, t):
        return remote(
            wr.at[j, 3, t], wr.at[j, 3, t], w_s.at[j, 1, t], w_r.at[j, 3, t], level(7)
        )

    def round_in(j, source, t):
        return remote(
            wr.at[j, source, t], wr.at[j, source, t], w_s.at[j, 0, t], w_r.at[j, source, t],
            level(7),
        )

    def extra(j, e, t):
        return remote(
            kv.at[j, 4 + e, t], kv.at[j, 4 + e, t], e_s.at[j, e, t], e_r.at[j, e, t], below
        )

    def down(j, d, t):
        return remote(
            rs.at[j, d, t], rr.at[j, d - 1, t], rd_s.at[j, d, t], rd_r.at[j, d - 1, t], below
        )

    def down_wide(j, d, t):
        return remote(
            rs_wide.at[j, d - 1, t], rr_wide.at[j, d - 1, t],
            rd_s.at[j, d, t], rd_r.at[j, d - 1, t], below,
        )

    def down_in(j, d, t):
        return remote(
            rr.at[j, d, t], rr.at[j, d, t], rd_s.at[j, d + 1, t], rd_r.at[j, d, t], below
        )

    def down_wide_in(j, d, t):
        return remote(
            rr_wide.at[j, d, t], rr_wide.at[j, d, t],
            rd_s.at[j, d + 1, t], rd_r.at[j, d, t], below,
        )

    def extra_back(j, e, t, target, way):
        return remote(es.at[j, e, t], er.at[j, e, t], er_s.at[j, way, t], er_r.at[j, e, t], target)

    def extra_on(j, t):
        return remote(er.at[j, 1, t], er.at[j, 1, t], er_s.at[j, 1, t], er_r.at[j, 1, t], level(3))

    def extra_in(j, e, t):
        return remote(er.at[j, e, t], er.at[j, e, t], er_s.at[j, e, t], er_r.at[j, e, t], above)

    def dq_swap(j):
        return remote(
            dq_out.at[j], dq_ref.at[0, :, lanes(xh * 2048 + j * 1024, 1024)],
            dq_s.at[j], dq_r.at[j], partner,
        )

    def dq_in(j):
        return remote(
            dq_out.at[j], dq_ref.at[0, :, lanes(xo * 2048 + j * 1024, 1024)],
            dq_s.at[j], dq_r.at[j], partner,
        )

    def hand_back(j, column):
        part = lanes(column * 2048 + j * 1024, 1024)
        return remote(
            dq_ref.at[0, :, part], hb_ref.at[0, :, part],
            hb_s.at[j, column], hb_r.at[j, column], before,
        )

    def fin_swap(j, t):
        dst = (dk_ref, dv_ref)[t]
        return remote(
            fin.at[j, t, rows(xo * ROWS, ROWS)],
            dst.at[0, :, lanes((2 * xh + j) * HD, HD)],
            f_s.at[j, t], f_r.at[j, t], partner,
        )

    def unit(j, r, d, first, masked=False):
        keys = kv[j, d, 0]
        values = kv[j, d, 1]
        d_keys = None
        d_values = None
        for c in range(8 // HEADS):
            base = j * 1024 + c * HEADS * HD
            head = j * 8 + c * HEADS
            queries = jnp.concatenate(
                [qa[r, :, base + i * HD : base + (i + 1) * HD] for i in range(HEADS)], axis=0
            )
            grads = jnp.concatenate(
                [ga[r, :, base + i * HD : base + (i + 1) * HD] for i in range(HEADS)], axis=0
            )
            lse = jnp.concatenate(
                [stat[0, r, pl.ds(head + i, 1), :] for i in range(HEADS)], axis=1
            )
            delta = jnp.concatenate(
                [stat[1, r, pl.ds(head + i, 1), :] for i in range(HEADS)], axis=1
            )
            scores = lax.dot_general(keys, queries, NT, preferred_element_type=F32)
            probs = jnp.exp2(scores * (SCALE * LOG2E) - lse)
            if masked:
                shape = (PAIR, HEADS * HD)
                key_at = lax.broadcasted_iota(jnp.int32, shape, 0)
                query_at = lax.broadcasted_iota(jnp.int32, shape, 1) % HD + r * ROWS
                probs = jnp.where(key_at <= query_at, probs, 0.0)
            prob_grads = lax.dot_general(values, grads, NT, preferred_element_type=F32)
            score_grads = (probs * (prob_grads - delta)).astype(BF16)
            probs_low = probs.astype(BF16)
            part_v = lax.dot_general(probs_low, grads, NN, preferred_element_type=F32)
            part_k = lax.dot_general(score_grads, queries, NN, preferred_element_type=F32)
            d_values = part_v if d_values is None else d_values + part_v
            d_keys = part_k if d_keys is None else d_keys + part_k
            dqt[r, :, base : base + HEADS * HD] += lax.dot_general(
                keys, score_grads, TN, preferred_element_type=F32
            )
        if first:
            acc[j, d, 0] = d_keys
            acc[j, d, 1] = d_values
        else:
            acc[j, d, 0] += d_keys
            acc[j, d, 1] += d_values

    def has(d):
        return (d <= chain) | (last_block & (d >= 4))

    def arrival(t):
        low = jnp.where((t > z) & (t <= 2 * z), 2 * z + 1 - t, 0)
        five = jnp.where(t == 6, 1, jnp.where(t > 6, 12 - t, 0))
        six = jnp.where(t == 3, 1, jnp.where(t == 7, 2, 0))
        seven = jnp.where(t == 3, 1, jnp.where(t == 4, 2, jnp.where(t == 8, 3, 0)))
        return jnp.where(
            z <= 4, low, jnp.where(z == 5, five, jnp.where(z == 6, six, seven))
        )

    def take(j, d):
        for t in range(2):
            up_in(j, d, t).wait_recv()

            @pl.when(d + 1 <= chain_above)
            def _():
                up(j, d, t).start()

    def choose(j, e):
        kv[j, 4 + e] = jnp.where(second, wr[j, 2 + e], wr[j, e])
        for t in range(2):
            extra(j, e, t).start()

    def extra_levels(j, k):
        @pl.when((z == 1) & (k == 2))
        def _():
            for t in range(2):
                round_in(j, 3, t).wait_recv()
                round_on(j, t).start()

        for e in range(2):
            @pl.when((z == 7) & (k == 3 + e))
            def _():
                for t in range(2):
                    round_in(j, e, t).wait_recv()
                    round_in(j, 2 + e, t).wait_recv()
                choose(j, e)

            @pl.when((z == 6) & (k == 4 + e))
            def _():
                for t in range(2):
                    extra(j, e, t).wait_recv()

    def gather(t):
        @pl.when(t <= chain)
        def _():
            take(0, t)

        slot = arrival(t)

        @pl.when(slot >= 1)
        def _():
            take(1, slot)

        at = jnp.where(z <= 3, jnp.maximum(2 * z, 1), jnp.where(z == 4, 4, 2))

        @pl.when((t == at) & (chain_above >= 1))
        def _():
            for kind in range(2):
                up(1, 0, kind).start()

        @pl.when((t == 3) & (z <= 3))
        def _():
            for kind in range(2):
                round_first(1, kind).start()

        extra_levels(0, t)
        extra_levels(1, t - 4)

    def starts_chain(d):
        return d + 1 > chain_above

    def send_first(j, d):
        @pl.when((d <= chain) & starts_chain(d))
        def _():
            for t in range(2):
                rs[j, d, t] = acc[j, d, t].astype(BF16)
                down(j, d, t).start()

        @pl.when((z == 6) & (d >= 4))
        def _():
            for t in range(2):
                es[j, d - 4, t] = acc[j, d, t].astype(BF16)
                extra_back(j, d - 4, t, above, d - 4).start()

    def send_on(j, d):
        due = (d >= 1) & (d <= chain) & jnp.logical_not(starts_chain(d))

        @pl.when(due & (z >= 3))
        def _():
            for t in range(2):
                down_in(j, d, t).wait_recv()
                rs[j, d, t] = (acc[j, d, t] + rr[j, d, t].astype(F32)).astype(BF16)
                down(j, d, t).start()

        @pl.when(due & (z == 2))
        def _():
            for t in range(2):
                down_in(j, d, t).wait_recv()
                rs_wide[j, d - 1, t] = acc[j, d, t] + rr[j, d, t].astype(F32)
                down_wide(j, d, t).start()

        @pl.when(due & (z == 1))
        def _():
            for t in range(2):
                down_wide_in(j, d, t).wait_recv()
                rs_wide[j, d - 1, t] = acc[j, d, t] + rr_wide[j, d, t]
                down_wide(j, d, t).start()

    def extra_sum(j, e):
        @pl.when(z == 7)
        def _():
            for t in range(2):
                extra_in(j, e, t).wait_recv()
                es[j, e, t] = (acc[j, 4 + e, t] + er[j, e, t].astype(F32)).astype(BF16)
                extra_back(j, e, t, level(e), e).start()
            if e == 1:
                for t in range(2):
                    extra_back(j, 0, t, level(2), 2).start()

    def extra_relay(j):
        @pl.when(z == 1)
        def _():
            for t in range(2):
                extra_in(j, 1, t).wait_recv()
                extra_on(j, t).start()

    def finish_keys(j):
        @pl.when(z <= 3)
        def _():
            e = z % 2

            @pl.when(z != 1)
            def _():
                for t in range(2):
                    extra_in(j, e, t).wait_recv()

            mine = second == (z >= 2)
            acc[j, 0] += jnp.where(mine, er[j, e].astype(F32), 0.0)

        for t in range(2):
            @pl.when((z >= 2) & (z <= 6))
            def _():
                down_in(j, 0, t).wait_recv()
                acc[j, 0, t] += rr[j, 0, t].astype(F32)

            @pl.when(z <= 1)
            def _():
                down_wide_in(j, 0, t).wait_recv()
                acc[j, 0, t] += rr_wide[j, 0, t]

            fin[j, t] = (acc[j, 0, t] * (SCALE if t == 0 else 1.0)).astype(BF16)
            fin_swap(j, t).start()
        columns = lanes((2 * xh + j) * HD, HD)
        dk_ref[0, :, columns] = fin[j, 0, rows(xh * ROWS, ROWS)]
        dv_ref[0, :, columns] = fin[j, 1, rows(xh * ROWS, ROWS)]

    def finish_queries(j):
        for i in range(8):
            cols = slice(j * 1024 + i * HD, j * 1024 + (i + 1) * HD)
            dq_out[j, :, i * HD : (i + 1) * HD] = (dqt[xo, :, cols].T * SCALE).astype(BF16)
        dq_swap(j).start()
        for i in range(8):
            cols = slice(j * 1024 + i * HD, j * 1024 + (i + 1) * HD)
            dq_ref[0, :, lanes(xh * 2048 + j * 1024 + i * HD, HD)] = (
                dqt[xh, :, cols].T * SCALE
            ).astype(BF16)

        @pl.when(pipe > 0)
        def _():
            hand_back(j, xh).start()

    def hand_on(j):
        dq_in(j).wait_recv()

        @pl.when(pipe > 0)
        def _():
            hand_back(j, xo).start()

    for j in range(2):
        for t in range(2):
            kv_own(j, t).start()
    for t in range(2):
        stat_own(t).start()
        for j in range(2):
            q_own(j, t).start()

    barrier = pltpu.get_barrier_semaphore()

    def greet(device):
        pl.semaphore_signal(barrier, inc=1, device_id=device, device_id_type=MESH)

    for device in (partner, above, below, before, after):
        greet(device)

    @pl.when((z == 1) | (z == 2))
    def _():
        greet(level(7))

    @pl.when(z == 7)
    def _():
        greet(level(1))
        greet(level(2))

    @pl.when(z == 1)
    def _():
        greet(level(3))

    @pl.when(z == 3)
    def _():
        greet(level(1))

    far_greetings = jnp.where((z == 1) | (z == 7), 2, jnp.where((z == 2) | (z == 3), 1, 0))
    pl.semaphore_wait(barrier, 5 + far_greetings)

    for j in range(2):
        for t in range(2):
            kv_swap(j, t).start()
        if j == 0:
            for t in range(2):
                stat_swap(t).start()

    dqt[...] = jnp.zeros_like(dqt)

    @pl.when(pipe == 15)
    def _():
        hb_ref[...] = jnp.zeros_like(hb_ref)

    for t in range(2):
        stat_own(t).wait()
    stat[0, xh] = stat_in[1, 0].astype(F32) * LOG2E
    stat[1, xh] = stat_in[1, 1].astype(F32)
    for j in range(2):
        for t in range(2):
            kv_own(j, t).wait()
            q_own(j, t).wait()

    for t in range(2):
        kv_swap(0, t).wait_recv()

        @pl.when(chain_above >= 1)
        def _():
            up(0, 0, t).start()

        @pl.when(z <= 3)
        def _():
            round_first(0, t).start()

    for j in range(2):
        for t in range(2):
            q_swap(j, t).start()
    for t in range(2):
        kv_swap(1, t).wait_recv()
        stat_swap(t).wait_recv()
    stat[0, xo] = stat_in[0, 0].astype(F32) * LOG2E
    stat[1, xo] = stat_in[0, 1].astype(F32)

    unit(0, xh, 0, True, True)

    def phase_a(k, carry):
        gather(k)

        @pl.when(has(k))
        def _():
            unit(0, xh, k, True)

        return carry

    unit(1, xh, 0, True, True)
    lax.fori_loop(1, 4, phase_a, 0)
    for t in range(2):
        q_swap(0, t).wait_recv()

    def arrived(k):
        return jnp.where(
            last_block, k, jnp.where(z == 5, jnp.where(k == 1, 1, 7 - k), chain + 1 - k)
        )

    def own_rows(k):
        d = arrived(k)

        @pl.when((d >= 1) & has(d))
        def _():
            unit(1, xh, d, True)

    def partner_rows(j, d):
        @pl.when((d >= 1) & has(d))
        def _():
            unit(j, xo, d, False)
            send_first(j, d)

    def phase_b(k, carry):
        phase_a(k, carry)
        partner_rows(0, k - 3)
        return carry

    lax.fori_loop(4, SLOTS, phase_b, 0)
    gather(6)

    def first_far(n, carry):
        partner_rows(0, 5 - n)
        return carry

    lax.fori_loop(0, 2, first_far, 0)
    own_rows(1)
    gather(7)
    partner_rows(0, 3)
    unit(0, xo, 0, False, True)
    finish_queries(0)
    own_rows(2)
    for t in range(2):
        q_swap(1, t).wait_recv()

    def phase_c(k, carry):
        gather(k + 5)
        own_rows(k)
        partner_rows(1, arrived(k - 2))
        for e in range(2):
            @pl.when(k == 3)
            def _():
                extra_sum(0, e)

        send_on(0, 7 - k)
        return carry

    lax.fori_loop(3, 6, phase_c, 0)
    hand_on(0)

    def phase_d(n, carry):
        partner_rows(1, arrived(4 + n))

        @pl.when(n == 0)
        def _():
            send_on(0, 1)
            send_on(1, 4)

        return carry

    lax.fori_loop(0, 2, phase_d, 0)
    extra_relay(0)
    unit(1, xo, 0, False, True)
    finish_queries(1)
    for e in range(2):
        extra_sum(1, e)

    def phase_e(k, carry):
        send_on(1, SLOTS - k)
        return carry

    lax.fori_loop(3, 4, phase_e, 0)
    finish_keys(0)
    hand_on(1)
    lax.fori_loop(4, SLOTS, phase_e, 0)
    extra_relay(1)
    finish_keys(1)

    for j in range(2):
        for t in range(2):
            fin_swap(j, t).wait_recv()
            fin_swap(j, t).wait_send()
            kv_swap(j, t).wait_send()
            q_swap(j, t).wait_send()
        dq_swap(j).wait_send()

        @pl.when(pipe > 0)
        def _():
            for column in range(2):
                hand_back(j, column).wait_send()

        @pl.when(pipe < 15)
        def _():
            for column in range(2):
                hand_back(j, column).wait_recv()

        for t in range(2):
            for d in range(SLOTS):
                @pl.when(d + 1 <= chain_above)
                def _():
                    up(j, d, t).wait_send()

                if d >= 1:
                    @pl.when((d <= chain) & (z >= 3))
                    def _():
                        down(j, d, t).wait_send()

                if d == 1 or d == 2:
                    @pl.when((d <= chain) & (z <= 2))
                    def _():
                        down_wide(j, d, t).wait_send()

            @pl.when(z <= 3)
            def _():
                round_first(j, t).wait_send()

            @pl.when(z == 1)
            def _():
                round_on(j, t).wait_send()
                extra_on(j, t).wait_send()

            for e in range(2):
                @pl.when(z == 7)
                def _():
                    extra(j, e, t).wait_send()

                @pl.when(last_block)
                def _():
                    extra_back(j, e, t, above, e).wait_send()

            @pl.when(z == 7)
            def _():
                extra_back(j, 0, t, level(2), 2).wait_send()

    for t in range(2):
        stat_swap(t).wait_send()


def write_out(*refs):
    done = refs[12]

    def piece(stage, i, c):
        part = pl.ds(c * 32, 32)
        return pltpu.make_async_copy(
            refs[(i, 8 + i)[stage]].at[0, part], refs[(8 + i, 4 + i)[stage]].at[0, part],
            done.at[stage, i, c],
        )

    pieces = [(i, c) for i in (0, 3, 1, 2) for c in range(4)]
    for i, c in pieces:
        piece(0, i, c).start()
    for i, c in pieces:
        piece(0, i, c).wait()
        piece(1, i, c).start()
    for i, c in pieces:
        piece(1, i, c).wait()


def per_device(queries, key_heads, value_heads, out_grad, log_sum, row_delta, chosen):
    vmem = pl.BlockSpec(memory_space=pltpu.VMEM)
    hbm = pl.BlockSpec(memory_space=pltpu.HBM)
    dma = pltpu.SemaphoreType.DMA
    level = (2, PAIR, HD)
    flops = 5 * 2 * ROWS * H * HD * 1536
    grads = pl.pallas_call(
        kernel,
        out_shape=(
            jax.ShapeDtypeStruct(queries.shape, BF16),
            jax.ShapeDtypeStruct(key_heads.shape, BF16),
            jax.ShapeDtypeStruct(value_heads.shape, BF16),
            jax.ShapeDtypeStruct(queries.shape, BF16),
        ),
        in_specs=[pl.BlockSpec(memory_space=pltpu.SMEM)] + [hbm] * 6,
        out_specs=(vmem,) * 4,
        scratch_shapes=[
            pltpu.VMEM((2, ROWS, 2048), BF16),
            pltpu.VMEM((2, ROWS, 2048), BF16),
            pltpu.VMEM((2, SLOTS) + level, BF16),
            pltpu.VMEM((2, 4) + level, BF16),
            pltpu.VMEM((2, SLOTS) + level, F32),
            pltpu.VMEM((2, HD, 2048), F32),
            pltpu.VMEM((2, 2, 16, ROWS), F32),
            pltpu.VMEM((2, 2, 16, ROWS), BF16),
            pltpu.VMEM((2, SLOTS) + level, BF16),
            pltpu.VMEM((2, SLOTS) + level, BF16),
            pltpu.VMEM((2, 2) + level, F32),
            pltpu.VMEM((2, 2) + level, F32),
            pltpu.VMEM((2, 2) + level, BF16),
            pltpu.VMEM((2, 2) + level, BF16),
            pltpu.VMEM((2, ROWS, 1024), BF16),
            pltpu.VMEM((2,) + level, BF16),
            dma((5, 2)),
            dma((3, 2)), dma((3, 2)),
            dma((2, 2)), dma((2, 2)),
            dma((2, SLOTS, 2)), dma((2, SLOTS, 2)),
            dma((2, 2, 2)), dma((2, 4, 2)),
            dma((2, 2, 2)), dma((2, 2, 2)),
            dma((2, SLOTS, 2)), dma((2, SLOTS, 2)),
            dma((2, 3, 2)), dma((2, 2, 2)),
            dma((2,)), dma((2,)),
            dma((2, 2)), dma((2, 2)),
            dma((2, 2)), dma((2, 2)),
        ],
        compiler_params=pltpu.CompilerParams(
            collective_id=0, has_side_effects=True, vmem_limit_bytes=63 * 2**20
        ),
        cost_estimate=pl.CostEstimate(
            flops=flops, bytes_accessed=6 * 2**20, transcendentals=ROWS * H * 1536
        ),
        name="block_attention_backward",
    )(chosen.transpose(0, 2, 1), queries, key_heads, value_heads, out_grad, log_sum, row_delta)
    anywhere = pl.BlockSpec(memory_space=pl.ANY)
    return pl.pallas_call(
        write_out,
        out_shape=tuple(jax.ShapeDtypeStruct(part.shape, part.dtype) for part in grads),
        in_specs=[anywhere] * 4,
        out_specs=(anywhere,) * 4,
        scratch_shapes=[pltpu.VMEM(part.shape, part.dtype) for part in grads] + [dma((2, 4, 4))],
        name="write_out",
    )(*grads)


def solution(mesh):
    heads = P("pipe", "ctx", None)
    stats = P("pipe", None, "ctx")
    return jax.shard_map(
        per_device,
        mesh=mesh,
        in_specs=(heads, heads, heads, heads, stats, stats, P("pipe", None, None)),
        out_specs=(heads, heads, heads, heads),
        check_vma=False,
    )
```

```python
import jax
import jax.numpy as jnp
from jax import lax
from jax.experimental import pallas as pl
from jax.experimental.pallas import tpu as pltpu
from jax.sharding import PartitionSpec as P

H = 32
KVH = 4
HD = 128
BLOCK = 512
ROWS = 128
PAIR = 2 * ROWS
SLOTS = 6
LEVELS = 8
LOG2E = 1.4426950408889634
SCALE = HD**-0.5
HEADS = 8
NT = (((1,), (1,)), ((), ()))
NN = (((1,), (0,)), ((), ()))
TN = (((0,), (0,)), ((), ()))
MESH = pl.DeviceIdType.MESH
F32 = jnp.float32
BF16 = jnp.bfloat16


def kernel(
    chosen_ref, q_ref, k_ref, v_ref, g_ref, lse_ref, delta_ref,
    dq_ref, dk_ref, dv_ref, hb_ref,
    qa, ga, kv, wr, acc, dqt, stat, stat_in, rs, rr, rs_wide, rr_wide, es, er, dq_out, fin,
    own_sem, x_s, x_r, qx_s, qx_r, first_s, up_s, up_r, w_s, w_r, e_s, e_r,
    rd_s, rd_r, er_s, er_r, dq_s, dq_r, hb_s, hb_r, f_s, f_r,
):
    pipe = lax.axis_index("pipe")
    place = lax.axis_index("ctx")
    z = place // 2
    xh = place % 2
    xo = 1 - xh

    def level(number):
        return (pipe, number * 2 + xh)

    partner = (pipe, z * 2 + xo)
    above = level((z + 1) % LEVELS)
    below = level((z + LEVELS - 1) % LEVELS)
    across_above = (pipe, ((z + 1) % LEVELS) * 2 + xo)
    across_below = (pipe, ((z + LEVELS - 1) % LEVELS) * 2 + xo)
    before = ((pipe + 15) % 16, place)
    after = ((pipe + 1) % 16, place)
    chain = jnp.where(z <= 5, z, z - 4)
    chain_above = jnp.where(z <= 4, z + 1, jnp.where(z == 7, 0, z - 3))
    last_block = z >= 6
    second = (chosen_ref[0, 0, 3] + chosen_ref[0, 1, 3]) == 3

    def remote(src, dst, send, recv, device):
        return pltpu.make_async_remote_copy(
            src_ref=src, dst_ref=dst, send_sem=send, recv_sem=recv,
            device_id=device, device_id_type=MESH,
        )

    def lanes(start, size):
        return pl.ds(pl.multiple_of(start, 128), size)

    def rows(start, size):
        return pl.ds(pl.multiple_of(start, 128), size)

    def kv_swap(j, t):
        src = (k_ref, v_ref)[t]
        return remote(
            src.at[0, :, lanes((2 * xo + j) * HD, HD)],
            kv.at[j, 0, t, rows(xh * ROWS, ROWS)],
            x_s.at[j, t], x_r.at[j, t], partner,
        )

    def kv_own(j, t):
        src = (k_ref, v_ref)[t]
        return pltpu.make_async_copy(
            src.at[0, :, lanes((2 * xh + j) * HD, HD)],
            kv.at[j, 0, t, rows(xh * ROWS, ROWS)],
            own_sem.at[j, t],
        )

    def q_swap(j, t):
        src, dst = ((q_ref, qa), (g_ref, ga))[t]
        return remote(
            src.at[0, :, lanes(xo * 2048 + j * 1024, 1024)],
            dst.at[xh, :, pl.ds(j * 1024, 1024)],
            qx_s.at[j, t], qx_r.at[j, t], partner,
        )

    def q_own(j, t):
        src, dst = ((q_ref, qa), (g_ref, ga))[t]
        return pltpu.make_async_copy(
            src.at[0, :, lanes(xh * 2048 + j * 1024, 1024)],
            dst.at[xh, :, pl.ds(j * 1024, 1024)],
            own_sem.at[2 + j, t],
        )

    def stat_swap(t):
        src = (lse_ref, delta_ref)[t]
        return remote(
            src.at[0, pl.ds(pl.multiple_of(xo * 16, 16), 16)],
            stat_in.at[0, t], x_s.at[2, t], x_r.at[2, t], partner,
        )

    def stat_own(t):
        src = (lse_ref, delta_ref)[t]
        return pltpu.make_async_copy(
            src.at[0, pl.ds(pl.multiple_of(xh * 16, 16), 16)],
            stat_in.at[1, t], own_sem.at[4, t],
        )

    def up(j, d, t):
        return remote(
            kv.at[j, d, t], kv.at[j, d + 1, t], up_s.at[j, d, t], up_r.at[j, d + 1, t], above
        )

    def first_up(t, column):
        src = (k_ref, v_ref)[t]
        heads = (xh, xo)[column]
        return remote(
            src.at[0, :, lanes(2 * heads * HD, HD)],
            kv.at[0, 1, t, rows(xh * ROWS, ROWS)],
            first_s.at[column, t], up_r.at[0, 1, t], (above, across_above)[column],
        )

    def up_in(j, d, t):
        return remote(
            kv.at[j, d - 1, t], kv.at[j, d, t], up_s.at[j, d - 1, t], up_r.at[j, d, t], above
        )

    def round_first(j, t):
        return remote(
            kv.at[j, 0, t], wr.at[j, z, t], w_s.at[j, 0, t], w_r.at[j, z, t],
            level(jnp.where(z == 3, 1, 7)),
        )

    def round_on(j, t):
        return remote(
            wr.at[j, 3, t], wr.at[j, 3, t], w_s.at[j, 1, t], w_r.at[j, 3, t], level(7)
        )

    def round_in(j, source, t):
        return remote(
            wr.at[j, source, t], wr.at[j, source, t], w_s.at[j, 0, t], w_r.at[j, source, t],
            level(7),
        )

    def extra(j, e, t):
        return remote(
            kv.at[j, 4 + e, t], kv.at[j, 4 + e, t], e_s.at[j, e, t], e_r.at[j, e, t], below
        )

    def down(j, d, t):
        return remote(
            rs.at[j, d, t], rr.at[j, d - 1, t], rd_s.at[j, d, t], rd_r.at[j, d - 1, t], below
        )

    def down_wide(j, d, t):
        return remote(
            rs_wide.at[j, d - 1, t], rr_wide.at[j, d - 1, t],
            rd_s.at[j, d, t], rd_r.at[j, d - 1, t], below,
        )

    def down_in(j, d, t):
        return remote(
            rr.at[j, d, t], rr.at[j, d, t], rd_s.at[j, d + 1, t], rd_r.at[j, d, t], below
        )

    def down_wide_in(j, d, t):
        return remote(
            rr_wide.at[j, d, t], rr_wide.at[j, d, t],
            rd_s.at[j, d + 1, t], rd_r.at[j, d, t], below,
        )

    def extra_back(j, e, t, target, way):
        return remote(es.at[j, e, t], er.at[j, e, t], er_s.at[j, way, t], er_r.at[j, e, t], target)

    def extra_on(j, t):
        return remote(er.at[j, 1, t], er.at[j, 1, t], er_s.at[j, 1, t], er_r.at[j, 1, t], level(3))

    def extra_in(j, e, t):
        return remote(er.at[j, e, t], er.at[j, e, t], er_s.at[j, e, t], er_r.at[j, e, t], above)

    def dq_swap(j):
        return remote(
            dq_out.at[j], dq_ref.at[0, :, lanes(xh * 2048 + j * 1024, 1024)],
            dq_s.at[j], dq_r.at[j], partner,
        )

    def dq_in(j):
        return remote(
            dq_out.at[j], dq_ref.at[0, :, lanes(xo * 2048 + j * 1024, 1024)],
            dq_s.at[j], dq_r.at[j], partner,
        )

    def hand_back(j, column):
        part = lanes(column * 2048 + j * 1024, 1024)
        return remote(
            dq_ref.at[0, :, part], hb_ref.at[0, :, part],
            hb_s.at[j, column], hb_r.at[j, column], before,
        )

    def fin_swap(j, t):
        dst = (dk_ref, dv_ref)[t]
        return remote(
            fin.at[j, t, rows(xo * ROWS, ROWS)],
            dst.at[0, :, lanes((2 * xh + j) * HD, HD)],
            f_s.at[j, t], f_r.at[j, t], partner,
        )

    def unit(j, r, d, first, masked=False):
        keys = kv[j, d, 0]
        values = kv[j, d, 1]
        d_keys = None
        d_values = None
        for c in range(8 // HEADS):
            base = j * 1024 + c * HEADS * HD
            head = j * 8 + c * HEADS
            queries = jnp.concatenate(
                [qa[r, :, base + i * HD : base + (i + 1) * HD] for i in range(HEADS)], axis=0
            )
            grads = jnp.concatenate(
                [ga[r, :, base + i * HD : base + (i + 1) * HD] for i in range(HEADS)], axis=0
            )
            lse = jnp.concatenate(
                [stat[0, r, pl.ds(head + i, 1), :] for i in range(HEADS)], axis=1
            )
            delta = jnp.concatenate(
                [stat[1, r, pl.ds(head + i, 1), :] for i in range(HEADS)], axis=1
            )
            scores = lax.dot_general(keys, queries, NT, preferred_element_type=F32)
            probs = jnp.exp2(scores * (SCALE * LOG2E) - lse)
            if masked:
                shape = (PAIR, HEADS * HD)
                key_at = lax.broadcasted_iota(jnp.int32, shape, 0)
                query_at = lax.broadcasted_iota(jnp.int32, shape, 1) % HD + r * ROWS
                probs = jnp.where(key_at <= query_at, probs, 0.0)
            prob_grads = lax.dot_general(values, grads, NT, preferred_element_type=F32)
            score_grads = (probs * (prob_grads - delta)).astype(BF16)
            probs_low = probs.astype(BF16)
            part_v = lax.dot_general(probs_low, grads, NN, preferred_element_type=F32)
            part_k = lax.dot_general(score_grads, queries, NN, preferred_element_type=F32)
            d_values = part_v if d_values is None else d_values + part_v
            d_keys = part_k if d_keys is None else d_keys + part_k
            dqt[r, :, base : base + HEADS * HD] += lax.dot_general(
                keys, score_grads, TN, preferred_element_type=F32
            )
        if first:
            acc[j, d, 0] = d_keys
            acc[j, d, 1] = d_values
        else:
            acc[j, d, 0] += d_keys
            acc[j, d, 1] += d_values

    def has(d):
        return (d <= chain) | (last_block & (d >= 4))

    def arrival(t):
        low = jnp.where((t > z) & (t <= 2 * z), 2 * z + 1 - t, 0)
        five = jnp.where(t == 6, 1, jnp.where(t > 6, 12 - t, 0))
        six = jnp.where(t == 3, 1, jnp.where(t == 7, 2, 0))
        seven = jnp.where(t == 3, 1, jnp.where(t == 4, 2, jnp.where(t == 8, 3, 0)))
        return jnp.where(
            z <= 4, low, jnp.where(z == 5, five, jnp.where(z == 6, six, seven))
        )

    def take(j, d):
        for t in range(2):
            up_in(j, d, t).wait_recv()

            @pl.when(d + 1 <= chain_above)
            def _():
                up(j, d, t).start()

    def choose(j, e):
        kv[j, 4 + e] = jnp.where(second, wr[j, 2 + e], wr[j, e])
        for t in range(2):
            extra(j, e, t).start()

    def extra_levels(j, k):
        @pl.when((z == 1) & (k == 2))
        def _():
            for t in range(2):
                round_in(j, 3, t).wait_recv()
                round_on(j, t).start()

        for e in range(2):
            @pl.when((z == 7) & (k == 3 + e))
            def _():
                for t in range(2):
                    round_in(j, e, t).wait_recv()
                    round_in(j, 2 + e, t).wait_recv()
                choose(j, e)

            @pl.when((z == 6) & (k == 4 + e))
            def _():
                for t in range(2):
                    extra(j, e, t).wait_recv()

    def gather(t):
        @pl.when(t <= chain)
        def _():
            take(0, t)

        slot = arrival(t)

        @pl.when(slot >= 1)
        def _():
            take(1, slot)

        at = jnp.where(z <= 3, jnp.maximum(2 * z, 1), jnp.where(z == 4, 4, 2))

        @pl.when((t == at) & (chain_above >= 1))
        def _():
            for kind in range(2):
                up(1, 0, kind).start()

        @pl.when((t == 3) & (z <= 3))
        def _():
            for kind in range(2):
                round_first(1, kind).start()

        extra_levels(0, t)
        extra_levels(1, t - 4)

    def starts_chain(d):
        return d + 1 > chain_above

    def send_first(j, d):
        @pl.when((d <= chain) & starts_chain(d))
        def _():
            for t in range(2):
                rs[j, d, t] = acc[j, d, t].astype(BF16)
                down(j, d, t).start()

        @pl.when((z == 6) & (d >= 4))
        def _():
            for t in range(2):
                es[j, d - 4, t] = acc[j, d, t].astype(BF16)
                extra_back(j, d - 4, t, above, d - 4).start()

    def send_on(j, d):
        due = (d >= 1) & (d <= chain) & jnp.logical_not(starts_chain(d))

        @pl.when(due & (z >= 3))
        def _():
            for t in range(2):
                down_in(j, d, t).wait_recv()
                rs[j, d, t] = (acc[j, d, t] + rr[j, d, t].astype(F32)).astype(BF16)
                down(j, d, t).start()

        @pl.when(due & (z == 2))
        def _():
            for t in range(2):
                down_in(j, d, t).wait_recv()
                rs_wide[j, d - 1, t] = acc[j, d, t] + rr[j, d, t].astype(F32)
                down_wide(j, d, t).start()

        @pl.when(due & (z == 1))
        def _():
            for t in range(2):
                down_wide_in(j, d, t).wait_recv()
                rs_wide[j, d - 1, t] = acc[j, d, t] + rr_wide[j, d, t]
                down_wide(j, d, t).start()

    def extra_sum(j, e):
        @pl.when(z == 7)
        def _():
            for t in range(2):
                extra_in(j, e, t).wait_recv()
                es[j, e, t] = (acc[j, 4 + e, t] + er[j, e, t].astype(F32)).astype(BF16)
                extra_back(j, e, t, level(e), e).start()
            if e == 1:
                for t in range(2):
                    extra_back(j, 0, t, level(2), 2).start()

    def extra_relay(j):
        @pl.when(z == 1)
        def _():
            for t in range(2):
                extra_in(j, 1, t).wait_recv()
                extra_on(j, t).start()

    def finish_keys(j):
        @pl.when(z <= 3)
        def _():
            e = z % 2

            @pl.when(z != 1)
            def _():
                for t in range(2):
                    extra_in(j, e, t).wait_recv()

            mine = second == (z >= 2)
            acc[j, 0] += jnp.where(mine, er[j, e].astype(F32), 0.0)

        for t in range(2):
            @pl.when((z >= 2) & (z <= 6))
            def _():
                down_in(j, 0, t).wait_recv()
                acc[j, 0, t] += rr[j, 0, t].astype(F32)

            @pl.when(z <= 1)
            def _():
                down_wide_in(j, 0, t).wait_recv()
                acc[j, 0, t] += rr_wide[j, 0, t]

            fin[j, t] = (acc[j, 0, t] * (SCALE if t == 0 else 1.0)).astype(BF16)
            fin_swap(j, t).start()
        columns = lanes((2 * xh + j) * HD, HD)
        dk_ref[0, :, columns] = fin[j, 0, rows(xh * ROWS, ROWS)]
        dv_ref[0, :, columns] = fin[j, 1, rows(xh * ROWS, ROWS)]

    def finish_queries(j):
        for i in range(8):
            cols = slice(j * 1024 + i * HD, j * 1024 + (i + 1) * HD)
            dq_out[j, :, i * HD : (i + 1) * HD] = (dqt[xo, :, cols].T * SCALE).astype(BF16)
        dq_swap(j).start()
        for i in range(8):
            cols = slice(j * 1024 + i * HD, j * 1024 + (i + 1) * HD)
            dq_ref[0, :, lanes(xh * 2048 + j * 1024 + i * HD, HD)] = (
                dqt[xh, :, cols].T * SCALE
            ).astype(BF16)

        @pl.when(pipe > 0)
        def _():
            hand_back(j, xh).start()

    def hand_on(j):
        dq_in(j).wait_recv()

        @pl.when(pipe > 0)
        def _():
            hand_back(j, xo).start()

    for j in range(2):
        for t in range(2):
            kv_own(j, t).start()
    for t in range(2):
        stat_own(t).start()
        for j in range(2):
            q_own(j, t).start()

    barrier = pltpu.get_barrier_semaphore()

    def greet(device):
        pl.semaphore_signal(barrier, inc=1, device_id=device, device_id_type=MESH)

    for device in (partner, above, below, across_above, across_below, before, after):
        greet(device)

    @pl.when((z == 1) | (z == 2))
    def _():
        greet(level(7))

    @pl.when(z == 7)
    def _():
        greet(level(1))
        greet(level(2))

    @pl.when(z == 1)
    def _():
        greet(level(3))

    @pl.when(z == 3)
    def _():
        greet(level(1))

    far_greetings = jnp.where((z == 1) | (z == 7), 2, jnp.where((z == 2) | (z == 3), 1, 0))
    pl.semaphore_wait(barrier, 7 + far_greetings)

    for j in range(2):
        for t in range(2):
            kv_swap(j, t).start()
            if j == 0:
                @pl.when(chain_above >= 1)
                def _():
                    for column in (1, 0):
                        first_up(t, column).start()

        if j == 0:
            for t in range(2):
                stat_swap(t).start()

    dqt[...] = jnp.zeros_like(dqt)

    @pl.when(pipe == 15)
    def _():
        hb_ref[...] = jnp.zeros_like(hb_ref)

    for t in range(2):
        stat_own(t).wait()
    stat[0, xh] = stat_in[1, 0].astype(F32) * LOG2E
    stat[1, xh] = stat_in[1, 1].astype(F32)
    for j in range(2):
        for t in range(2):
            kv_own(j, t).wait()
            q_own(j, t).wait()

    for t in range(2):
        kv_swap(0, t).wait_recv()

        @pl.when(z <= 3)
        def _():
            round_first(0, t).start()

    for j in range(2):
        for t in range(2):
            q_swap(j, t).start()
    for t in range(2):
        kv_swap(1, t).wait_recv()
        stat_swap(t).wait_recv()
    stat[0, xo] = stat_in[0, 0].astype(F32) * LOG2E
    stat[1, xo] = stat_in[0, 1].astype(F32)

    unit(0, xh, 0, True, True)

    def phase_a(k, carry):
        gather(k)

        @pl.when(has(k))
        def _():
            unit(0, xh, k, True)

        return carry

    unit(1, xh, 0, True, True)
    lax.fori_loop(1, 4, phase_a, 0)
    for t in range(2):
        q_swap(0, t).wait_recv()

    def arrived(k):
        return jnp.where(
            last_block, k, jnp.where(z == 5, jnp.where(k == 1, 1, 7 - k), chain + 1 - k)
        )

    def own_rows(k):
        d = arrived(k)

        @pl.when((d >= 1) & has(d))
        def _():
            unit(1, xh, d, True)

    def partner_rows(j, d):
        @pl.when((d >= 1) & has(d))
        def _():
            unit(j, xo, d, False)
            send_first(j, d)

    def phase_b(k, carry):
        phase_a(k, carry)
        partner_rows(0, k - 3)
        return carry

    lax.fori_loop(4, SLOTS, phase_b, 0)
    gather(6)

    def first_far(n, carry):
        partner_rows(0, 5 - n)
        return carry

    lax.fori_loop(0, 2, first_far, 0)
    own_rows(1)
    gather(7)
    partner_rows(0, 3)
    unit(0, xo, 0, False, True)
    finish_queries(0)
    own_rows(2)
    for t in range(2):
        q_swap(1, t).wait_recv()

    def phase_c(k, carry):
        gather(k + 5)
        own_rows(k)
        partner_rows(1, arrived(k - 2))
        for e in range(2):
            @pl.when(k == 3)
            def _():
                extra_sum(0, e)

        send_on(0, 7 - k)
        return carry

    lax.fori_loop(3, 6, phase_c, 0)
    hand_on(0)

    def phase_d(n, carry):
        partner_rows(1, arrived(4 + n))

        @pl.when(n == 0)
        def _():
            send_on(0, 1)
            send_on(1, 4)

        return carry

    lax.fori_loop(0, 2, phase_d, 0)
    extra_relay(0)
    unit(1, xo, 0, False, True)
    finish_queries(1)
    for e in range(2):
        extra_sum(1, e)

    def phase_e(k, carry):
        send_on(1, SLOTS - k)
        return carry

    lax.fori_loop(3, 5, phase_e, 0)
    finish_keys(0)
    hand_on(1)
    lax.fori_loop(5, SLOTS, phase_e, 0)
    extra_relay(1)
    finish_keys(1)

    for j in range(2):
        for t in range(2):
            fin_swap(j, t).wait_recv()
            fin_swap(j, t).wait_send()
            kv_swap(j, t).wait_send()
            q_swap(j, t).wait_send()
        dq_swap(j).wait_send()

        @pl.when(pipe > 0)
        def _():
            for column in range(2):
                hand_back(j, column).wait_send()

        @pl.when(pipe < 15)
        def _():
            for column in range(2):
                hand_back(j, column).wait_recv()

        for t in range(2):
            for d in range(SLOTS):
                @pl.when(d + 1 <= chain_above)
                def _():
                    if j == 0 and d == 0:
                        for column in range(2):
                            first_up(t, column).wait_send()
                    else:
                        up(j, d, t).wait_send()

                if d >= 1:
                    @pl.when((d <= chain) & (z >= 3))
                    def _():
                        down(j, d, t).wait_send()

                if d == 1 or d == 2:
                    @pl.when((d <= chain) & (z <= 2))
                    def _():
                        down_wide(j, d, t).wait_send()

            @pl.when(z <= 3)
            def _():
                round_first(j, t).wait_send()

            @pl.when(z == 1)
            def _():
                round_on(j, t).wait_send()
                extra_on(j, t).wait_send()

            for e in range(2):
                @pl.when(z == 7)
                def _():
                    extra(j, e, t).wait_send()

                @pl.when(last_block)
                def _():
                    extra_back(j, e, t, above, e).wait_send()

            @pl.when(z == 7)
            def _():
                extra_back(j, 0, t, level(2), 2).wait_send()

    for t in range(2):
        stat_swap(t).wait_send()


def write_out(*refs):
    done = refs[12]

    def piece(stage, i, c):
        part = pl.ds(c * 32, 32)
        return pltpu.make_async_copy(
            refs[(i, 8 + i)[stage]].at[0, part], refs[(8 + i, 4 + i)[stage]].at[0, part],
            done.at[stage, i, c],
        )

    pieces = [(i, c) for i in (0, 3, 1, 2) for c in range(4)]
    for i, c in pieces:
        piece(0, i, c).start()
    for i, c in pieces:
        piece(0, i, c).wait()
        piece(1, i, c).start()
    for i, c in pieces:
        piece(1, i, c).wait()


def per_device(queries, key_heads, value_heads, out_grad, log_sum, row_delta, chosen):
    vmem = pl.BlockSpec(memory_space=pltpu.VMEM)
    hbm = pl.BlockSpec(memory_space=pltpu.HBM)
    dma = pltpu.SemaphoreType.DMA
    level = (2, PAIR, HD)
    flops = 5 * 2 * ROWS * H * HD * 1536
    grads = pl.pallas_call(
        kernel,
        out_shape=(
            jax.ShapeDtypeStruct(queries.shape, BF16),
            jax.ShapeDtypeStruct(key_heads.shape, BF16),
            jax.ShapeDtypeStruct(value_heads.shape, BF16),
            jax.ShapeDtypeStruct(queries.shape, BF16),
        ),
        in_specs=[pl.BlockSpec(memory_space=pltpu.SMEM)] + [hbm] * 6,
        out_specs=(vmem,) * 4,
        scratch_shapes=[
            pltpu.VMEM((2, ROWS, 2048), BF16),
            pltpu.VMEM((2, ROWS, 2048), BF16),
            pltpu.VMEM((2, SLOTS) + level, BF16),
            pltpu.VMEM((2, 4) + level, BF16),
            pltpu.VMEM((2, SLOTS) + level, F32),
            pltpu.VMEM((2, HD, 2048), F32),
            pltpu.VMEM((2, 2, 16, ROWS), F32),
            pltpu.VMEM((2, 2, 16, ROWS), BF16),
            pltpu.VMEM((2, SLOTS) + level, BF16),
            pltpu.VMEM((2, SLOTS) + level, BF16),
            pltpu.VMEM((2, 2) + level, F32),
            pltpu.VMEM((2, 2) + level, F32),
            pltpu.VMEM((2, 2) + level, BF16),
            pltpu.VMEM((2, 2) + level, BF16),
            pltpu.VMEM((2, ROWS, 1024), BF16),
            pltpu.VMEM((2,) + level, BF16),
            dma((5, 2)),
            dma((3, 2)), dma((3, 2)),
            dma((2, 2)), dma((2, 2)),
            dma((2, 2)),
            dma((2, SLOTS, 2)), dma((2, SLOTS, 2)),
            dma((2, 2, 2)), dma((2, 4, 2)),
            dma((2, 2, 2)), dma((2, 2, 2)),
            dma((2, SLOTS, 2)), dma((2, SLOTS, 2)),
            dma((2, 3, 2)), dma((2, 2, 2)),
            dma((2,)), dma((2,)),
            dma((2, 2)), dma((2, 2)),
            dma((2, 2)), dma((2, 2)),
        ],
        compiler_params=pltpu.CompilerParams(
            collective_id=0, has_side_effects=True, vmem_limit_bytes=63 * 2**20
        ),
        cost_estimate=pl.CostEstimate(
            flops=flops, bytes_accessed=6 * 2**20, transcendentals=ROWS * H * 1536
        ),
        name="block_attention_backward",
    )(chosen.transpose(0, 2, 1), queries, key_heads, value_heads, out_grad, log_sum, row_delta)
    anywhere = pl.BlockSpec(memory_space=pl.ANY)
    return pl.pallas_call(
        write_out,
        out_shape=tuple(jax.ShapeDtypeStruct(part.shape, part.dtype) for part in grads),
        in_specs=[anywhere] * 4,
        out_specs=(anywhere,) * 4,
        scratch_shapes=[pltpu.VMEM(part.shape, part.dtype) for part in grads] + [dma((2, 4, 4))],
        name="write_out",
    )(*grads)


def solution(mesh):
    heads = P("pipe", "ctx", None)
    stats = P("pipe", None, "ctx")
    return jax.shard_map(
        per_device,
        mesh=mesh,
        in_specs=(heads, heads, heads, heads, stats, stats, P("pipe", None, None)),
        out_specs=(heads, heads, heads, heads),
        check_vma=False,
    )
```

```python
import jax
import jax.numpy as jnp
from jax import lax
from jax.experimental import pallas as pl
from jax.experimental.pallas import tpu as pltpu
from jax.sharding import PartitionSpec as P

H = 32
KVH = 4
HD = 128
BLOCK = 512
ROWS = 128
PAIR = 2 * ROWS
SLOTS = 6
LEVELS = 8
LOG2E = 1.4426950408889634
SCALE = HD**-0.5
HEADS = 8
NT = (((1,), (1,)), ((), ()))
NN = (((1,), (0,)), ((), ()))
TN = (((0,), (0,)), ((), ()))
MESH = pl.DeviceIdType.MESH
F32 = jnp.float32
BF16 = jnp.bfloat16


def kernel(
    chosen_ref, q_ref, k_ref, v_ref, g_ref, lse_ref, delta_ref,
    dq_ref, dk_ref, dv_ref, hb_ref,
    qa, ga, kv, wr, acc, dqt, stat, stat_in, rs, rr, rs_wide, rr_wide, es, er, dq_out, fin,
    own_sem, x_s, x_r, qx_s, qx_r, first_s, up_s, up_r, w_s, w_r, e_s, e_r,
    rd_s, rd_r, er_s, er_r, dq_s, dq_r, hb_s, hb_r, f_s, f_r,
):
    pipe = lax.axis_index("pipe")
    place = lax.axis_index("ctx")
    z = place // 2
    xh = place % 2
    xo = 1 - xh

    def level(number):
        return (pipe, number * 2 + xh)

    partner = (pipe, z * 2 + xo)
    above = level((z + 1) % LEVELS)
    below = level((z + LEVELS - 1) % LEVELS)
    across_above = (pipe, ((z + 1) % LEVELS) * 2 + xo)
    across_below = (pipe, ((z + LEVELS - 1) % LEVELS) * 2 + xo)
    before = ((pipe + 15) % 16, place)
    after = ((pipe + 1) % 16, place)
    chain = jnp.where(z <= 5, z, z - 4)
    chain_above = jnp.where(z <= 4, z + 1, jnp.where(z == 7, 0, z - 3))
    last_block = z >= 6
    second = (chosen_ref[0, 0, 3] + chosen_ref[0, 1, 3]) == 3

    def remote(src, dst, send, recv, device):
        return pltpu.make_async_remote_copy(
            src_ref=src, dst_ref=dst, send_sem=send, recv_sem=recv,
            device_id=device, device_id_type=MESH,
        )

    def lanes(start, size):
        return pl.ds(pl.multiple_of(start, 128), size)

    def rows(start, size):
        return pl.ds(pl.multiple_of(start, 128), size)

    def kv_swap(j, t):
        src = (k_ref, v_ref)[t]
        return remote(
            src.at[0, :, lanes((2 * xo + j) * HD, HD)],
            kv.at[j, 0, t, rows(xh * ROWS, ROWS)],
            x_s.at[j, t], x_r.at[j, t], partner,
        )

    def kv_own(j, t):
        src = (k_ref, v_ref)[t]
        return pltpu.make_async_copy(
            src.at[0, :, lanes((2 * xh + j) * HD, HD)],
            kv.at[j, 0, t, rows(xh * ROWS, ROWS)],
            own_sem.at[j, t],
        )

    def q_swap(j, t):
        src, dst = ((q_ref, qa), (g_ref, ga))[t]
        return remote(
            src.at[0, :, lanes(xo * 2048 + j * 1024, 1024)],
            dst.at[xh, :, pl.ds(j * 1024, 1024)],
            qx_s.at[j, t], qx_r.at[j, t], partner,
        )

    def q_own(j, t):
        src, dst = ((q_ref, qa), (g_ref, ga))[t]
        return pltpu.make_async_copy(
            src.at[0, :, lanes(xh * 2048 + j * 1024, 1024)],
            dst.at[xh, :, pl.ds(j * 1024, 1024)],
            own_sem.at[2 + j, t],
        )

    def stat_swap(t):
        src = (lse_ref, delta_ref)[t]
        return remote(
            src.at[0, pl.ds(pl.multiple_of(xo * 16, 16), 16)],
            stat_in.at[0, t], x_s.at[2, t], x_r.at[2, t], partner,
        )

    def stat_own(t):
        src = (lse_ref, delta_ref)[t]
        return pltpu.make_async_copy(
            src.at[0, pl.ds(pl.multiple_of(xh * 16, 16), 16)],
            stat_in.at[1, t], own_sem.at[4, t],
        )

    def up(j, d, t):
        return remote(
            kv.at[j, d, t], kv.at[j, d + 1, t], up_s.at[j, d, t], up_r.at[j, d + 1, t], above
        )

    def first_up(t, column):
        src = (k_ref, v_ref)[t]
        heads = (xh, xo)[column]
        return remote(
            src.at[0, :, lanes(2 * heads * HD, HD)],
            kv.at[0, 1, t, rows(xh * ROWS, ROWS)],
            first_s.at[column, t], up_r.at[0, 1, t], (above, across_above)[column],
        )

    def up_in(j, d, t):
        return remote(
            kv.at[j, d - 1, t], kv.at[j, d, t], up_s.at[j, d - 1, t], up_r.at[j, d, t], above
        )

    def round_first(j, t):
        return remote(
            kv.at[j, 0, t], wr.at[j, z, t], w_s.at[j, 0, t], w_r.at[j, z, t],
            level(jnp.where(z == 3, 1, 7)),
        )

    def round_on(j, t):
        return remote(
            wr.at[j, 3, t], wr.at[j, 3, t], w_s.at[j, 1, t], w_r.at[j, 3, t], level(7)
        )

    def round_in(j, source, t):
        return remote(
            wr.at[j, source, t], wr.at[j, source, t], w_s.at[j, 0, t], w_r.at[j, source, t],
            level(7),
        )

    def extra(j, e, t):
        return remote(
            kv.at[j, 4 + e, t], kv.at[j, 4 + e, t], e_s.at[j, e, t], e_r.at[j, e, t], below
        )

    def down(j, d, t):
        return remote(
            rs.at[j, d, t], rr.at[j, d - 1, t], rd_s.at[j, d, t], rd_r.at[j, d - 1, t], below
        )

    def down_wide(j, d, t):
        return remote(
            rs_wide.at[j, d - 1, t], rr_wide.at[j, d - 1, t],
            rd_s.at[j, d, t], rd_r.at[j, d - 1, t], below,
        )

    def down_in(j, d, t):
        return remote(
            rr.at[j, d, t], rr.at[j, d, t], rd_s.at[j, d + 1, t], rd_r.at[j, d, t], below
        )

    def down_wide_in(j, d, t):
        return remote(
            rr_wide.at[j, d, t], rr_wide.at[j, d, t],
            rd_s.at[j, d + 1, t], rd_r.at[j, d, t], below,
        )

    def extra_back(j, e, t, target, way):
        return remote(es.at[j, e, t], er.at[j, e, t], er_s.at[j, way, t], er_r.at[j, e, t], target)

    def extra_on(j, t):
        return remote(er.at[j, 1, t], er.at[j, 1, t], er_s.at[j, 1, t], er_r.at[j, 1, t], level(3))

    def extra_in(j, e, t):
        return remote(er.at[j, e, t], er.at[j, e, t], er_s.at[j, e, t], er_r.at[j, e, t], above)

    def dq_swap(j):
        return remote(
            dq_out.at[j], dq_ref.at[0, :, lanes(xh * 2048 + j * 1024, 1024)],
            dq_s.at[j], dq_r.at[j], partner,
        )

    def dq_in(j):
        return remote(
            dq_out.at[j], dq_ref.at[0, :, lanes(xo * 2048 + j * 1024, 1024)],
            dq_s.at[j], dq_r.at[j], partner,
        )

    def hand_back(j, column):
        part = lanes(column * 2048 + j * 1024, 1024)
        return remote(
            dq_ref.at[0, :, part], hb_ref.at[0, :, part],
            hb_s.at[j, column], hb_r.at[j, column], before,
        )

    def fin_swap(j, t):
        dst = (dk_ref, dv_ref)[t]
        return remote(
            fin.at[j, t, rows(xo * ROWS, ROWS)],
            dst.at[0, :, lanes((2 * xh + j) * HD, HD)],
            f_s.at[j, t], f_r.at[j, t], partner,
        )

    def unit(j, r, d, first, masked=False):
        keys = kv[j, d, 0]
        values = kv[j, d, 1]
        d_keys = None
        d_values = None
        for c in range(8 // HEADS):
            base = j * 1024 + c * HEADS * HD
            head = j * 8 + c * HEADS
            queries = jnp.concatenate(
                [qa[r, :, base + i * HD : base + (i + 1) * HD] for i in range(HEADS)], axis=0
            )
            grads = jnp.concatenate(
                [ga[r, :, base + i * HD : base + (i + 1) * HD] for i in range(HEADS)], axis=0
            )
            lse = jnp.concatenate(
                [stat[0, r, pl.ds(head + i, 1), :] for i in range(HEADS)], axis=1
            )
            delta = jnp.concatenate(
                [stat[1, r, pl.ds(head + i, 1), :] for i in range(HEADS)], axis=1
            )
            scores = lax.dot_general(keys, queries, NT, preferred_element_type=F32)
            probs = jnp.exp2(scores * (SCALE * LOG2E) - lse)
            if masked:
                shape = (PAIR, HEADS * HD)
                key_at = lax.broadcasted_iota(jnp.int32, shape, 0)
                query_at = lax.broadcasted_iota(jnp.int32, shape, 1) % HD + r * ROWS
                probs = jnp.where(key_at <= query_at, probs, 0.0)
            prob_grads = lax.dot_general(values, grads, NT, preferred_element_type=F32)
            score_grads = (probs * (prob_grads - delta)).astype(BF16)
            probs_low = probs.astype(BF16)
            part_v = lax.dot_general(probs_low, grads, NN, preferred_element_type=F32)
            part_k = lax.dot_general(score_grads, queries, NN, preferred_element_type=F32)
            d_values = part_v if d_values is None else d_values + part_v
            d_keys = part_k if d_keys is None else d_keys + part_k
            dqt[r, :, base : base + HEADS * HD] += lax.dot_general(
                keys, score_grads, TN, preferred_element_type=F32
            )
        if first:
            acc[j, d, 0] = d_keys
            acc[j, d, 1] = d_values
        else:
            acc[j, d, 0] += d_keys
            acc[j, d, 1] += d_values

    def has(d):
        return (d <= chain) | (last_block & (d >= 4))

    def arrival(t):
        low = jnp.where((t > z) & (t <= 2 * z), 2 * z + 1 - t, 0)
        five = jnp.where(t == 6, 1, jnp.where(t > 6, 12 - t, 0))
        six = jnp.where(t == 3, 1, jnp.where(t == 7, 2, 0))
        seven = jnp.where(t == 3, 1, jnp.where(t == 4, 2, jnp.where(t == 8, 3, 0)))
        return jnp.where(
            z <= 4, low, jnp.where(z == 5, five, jnp.where(z == 6, six, seven))
        )

    def take(j, d):
        for t in range(2):
            up_in(j, d, t).wait_recv()

            @pl.when(d + 1 <= chain_above)
            def _():
                up(j, d, t).start()

    def choose(j, e):
        kv[j, 4 + e] = jnp.where(second, wr[j, 2 + e], wr[j, e])
        for t in range(2):
            extra(j, e, t).start()

    def extra_levels(j, k):
        @pl.when((z == 1) & (k == 2))
        def _():
            for t in range(2):
                round_in(j, 3, t).wait_recv()
                round_on(j, t).start()

        for e in range(2):
            @pl.when((z == 7) & (k == 3 + e))
            def _():
                for t in range(2):
                    round_in(j, e, t).wait_recv()
                    round_in(j, 2 + e, t).wait_recv()
                choose(j, e)

            @pl.when((z == 6) & (k == 4 + e))
            def _():
                for t in range(2):
                    extra(j, e, t).wait_recv()

    def gather(t):
        @pl.when(t <= chain)
        def _():
            take(0, t)

        slot = arrival(t)

        @pl.when(slot >= 1)
        def _():
            take(1, slot)

        at = jnp.where(z <= 3, jnp.maximum(2 * z, 1), jnp.where(z == 4, 4, 2))

        @pl.when((t == at) & (chain_above >= 1))
        def _():
            for kind in range(2):
                up(1, 0, kind).start()

        @pl.when((t == 3) & (z <= 3))
        def _():
            for kind in range(2):
                round_first(1, kind).start()

        extra_levels(0, t)
        extra_levels(1, t - 4)

    def starts_chain(d):
        return d + 1 > chain_above

    def send_first(j, d):
        @pl.when((d <= chain) & starts_chain(d))
        def _():
            for t in range(2):
                rs[j, d, t] = acc[j, d, t].astype(BF16)
                down(j, d, t).start()

        @pl.when((z == 6) & (d >= 4))
        def _():
            for t in range(2):
                es[j, d - 4, t] = acc[j, d, t].astype(BF16)
                extra_back(j, d - 4, t, above, d - 4).start()

    def send_on(j, d):
        due = (d >= 1) & (d <= chain) & jnp.logical_not(starts_chain(d))

        @pl.when(due & (z >= 3))
        def _():
            for t in range(2):
                down_in(j, d, t).wait_recv()
                rs[j, d, t] = (acc[j, d, t] + rr[j, d, t].astype(F32)).astype(BF16)
                down(j, d, t).start()

        @pl.when(due & (z == 2))
        def _():
            for t in range(2):
                down_in(j, d, t).wait_recv()
                rs_wide[j, d - 1, t] = acc[j, d, t] + rr[j, d, t].astype(F32)
                down_wide(j, d, t).start()

        @pl.when(due & (z == 1))
        def _():
            for t in range(2):
                down_wide_in(j, d, t).wait_recv()
                rs_wide[j, d - 1, t] = acc[j, d, t] + rr_wide[j, d, t]
                down_wide(j, d, t).start()

    def extra_sum(j, e):
        @pl.when(z == 7)
        def _():
            for t in range(2):
                extra_in(j, e, t).wait_recv()
                es[j, e, t] = (acc[j, 4 + e, t] + er[j, e, t].astype(F32)).astype(BF16)
                extra_back(j, e, t, level(e), e).start()
            if e == 1:
                for t in range(2):
                    extra_back(j, 0, t, level(2), 2).start()

    def extra_relay(j):
        @pl.when(z == 1)
        def _():
            for t in range(2):
                extra_in(j, 1, t).wait_recv()
                extra_on(j, t).start()

    def finish_keys(j):
        @pl.when(z <= 3)
        def _():
            e = z % 2

            @pl.when(z != 1)
            def _():
                for t in range(2):
                    extra_in(j, e, t).wait_recv()

            mine = second == (z >= 2)
            acc[j, 0] += jnp.where(mine, er[j, e].astype(F32), 0.0)

        for t in range(2):
            @pl.when((z >= 2) & (z <= 6))
            def _():
                down_in(j, 0, t).wait_recv()
                acc[j, 0, t] += rr[j, 0, t].astype(F32)

            @pl.when(z <= 1)
            def _():
                down_wide_in(j, 0, t).wait_recv()
                acc[j, 0, t] += rr_wide[j, 0, t]

            fin[j, t] = (acc[j, 0, t] * (SCALE if t == 0 else 1.0)).astype(BF16)
            fin_swap(j, t).start()
        columns = lanes((2 * xh + j) * HD, HD)
        dk_ref[0, :, columns] = fin[j, 0, rows(xh * ROWS, ROWS)]
        dv_ref[0, :, columns] = fin[j, 1, rows(xh * ROWS, ROWS)]

    def finish_queries(j):
        for i in range(8):
            cols = slice(j * 1024 + i * HD, j * 1024 + (i + 1) * HD)
            dq_out[j, :, i * HD : (i + 1) * HD] = (dqt[xo, :, cols].T * SCALE).astype(BF16)
        dq_swap(j).start()
        for i in range(8):
            cols = slice(j * 1024 + i * HD, j * 1024 + (i + 1) * HD)
            dq_ref[0, :, lanes(xh * 2048 + j * 1024 + i * HD, HD)] = (
                dqt[xh, :, cols].T * SCALE
            ).astype(BF16)

        @pl.when(pipe > 0)
        def _():
            hand_back(j, xh).start()

    def hand_on(j):
        dq_in(j).wait_recv()

        @pl.when(pipe > 0)
        def _():
            hand_back(j, xo).start()

    for j in range(2):
        for t in range(2):
            kv_own(j, t).start()
    for t in range(2):
        stat_own(t).start()
        for j in range(2):
            q_own(j, t).start()

    barrier = pltpu.get_barrier_semaphore()

    def greet(device):
        pl.semaphore_signal(barrier, inc=1, device_id=device, device_id_type=MESH)

    for device in (partner, above, below, across_above, across_below, before, after):
        greet(device)

    @pl.when((z == 1) | (z == 2))
    def _():
        greet(level(7))

    @pl.when(z == 7)
    def _():
        greet(level(1))
        greet(level(2))

    @pl.when(z == 1)
    def _():
        greet(level(3))

    @pl.when(z == 3)
    def _():
        greet(level(1))

    far_greetings = jnp.where((z == 1) | (z == 7), 2, jnp.where((z == 2) | (z == 3), 1, 0))
    pl.semaphore_wait(barrier, 7 + far_greetings)

    for j in range(2):
        for t in range(2):
            kv_swap(j, t).start()
            if j == 0:
                @pl.when(chain_above >= 1)
                def _():
                    for column in (1, 0):
                        first_up(t, column).start()

        if j == 0:
            for t in range(2):
                stat_swap(t).start()

    dqt[...] = jnp.zeros_like(dqt)

    @pl.when(pipe == 15)
    def _():
        hb_ref[...] = jnp.zeros_like(hb_ref)

    for t in range(2):
        stat_own(t).wait()
    stat[0, xh] = stat_in[1, 0].astype(F32) * LOG2E
    stat[1, xh] = stat_in[1, 1].astype(F32)
    for j in range(2):
        for t in range(2):
            kv_own(j, t).wait()
            q_own(j, t).wait()

    for t in range(2):
        kv_swap(0, t).wait_recv()

        @pl.when(z <= 3)
        def _():
            round_first(0, t).start()

    for j in range(2):
        for t in range(2):
            q_swap(j, t).start()
    for t in range(2):
        kv_swap(1, t).wait_recv()
        stat_swap(t).wait_recv()
    stat[0, xo] = stat_in[0, 0].astype(F32) * LOG2E
    stat[1, xo] = stat_in[0, 1].astype(F32)

    unit(0, xh, 0, True, True)

    def phase_a(k, carry):
        gather(k)

        @pl.when(has(k))
        def _():
            unit(0, xh, k, True)

        return carry

    unit(1, xh, 0, True, True)
    lax.fori_loop(1, 4, phase_a, 0)
    for t in range(2):
        q_swap(0, t).wait_recv()

    def arrived(k):
        return jnp.where(
            last_block, k, jnp.where(z == 5, jnp.where(k == 1, 1, 7 - k), chain + 1 - k)
        )

    def own_rows(k):
        d = arrived(k)

        @pl.when((d >= 1) & has(d))
        def _():
            unit(1, xh, d, True)

    def partner_rows(j, d):
        @pl.when((d >= 1) & has(d))
        def _():
            unit(j, xo, d, False)
            send_first(j, d)

    def phase_b(k, carry):
        phase_a(k, carry)
        partner_rows(0, k - 3)
        return carry

    lax.fori_loop(4, SLOTS, phase_b, 0)
    gather(6)

    def first_far(n, carry):
        partner_rows(0, 5 - n)
        return carry

    lax.fori_loop(0, 2, first_far, 0)
    own_rows(1)
    gather(7)
    partner_rows(0, 3)
    unit(0, xo, 0, False, True)
    finish_queries(0)
    own_rows(2)
    for t in range(2):
        q_swap(1, t).wait_recv()

    def phase_c(k, carry):
        gather(k + 5)
        own_rows(k)
        partner_rows(1, arrived(k - 2))
        for e in range(2):
            @pl.when(k == 3)
            def _():
                extra_sum(0, e)

        send_on(0, 7 - k)
        return carry

    lax.fori_loop(3, 6, phase_c, 0)
    hand_on(0)

    def phase_d(n, carry):
        partner_rows(1, arrived(4 + n))

        @pl.when(n == 0)
        def _():
            send_on(0, 1)
            send_on(1, 4)

        return carry

    lax.fori_loop(0, 2, phase_d, 0)
    extra_relay(0)
    unit(1, xo, 0, False, True)
    finish_queries(1)
    for e in range(2):
        extra_sum(1, e)

    def phase_e(k, carry):
        send_on(1, SLOTS - k)
        return carry

    lax.fori_loop(3, 5, phase_e, 0)
    finish_keys(0)
    hand_on(1)
    lax.fori_loop(5, SLOTS, phase_e, 0)
    extra_relay(1)
    finish_keys(1)

    for j in range(2):
        for t in range(2):
            fin_swap(j, t).wait_recv()
            fin_swap(j, t).wait_send()
            kv_swap(j, t).wait_send()
            q_swap(j, t).wait_send()
        dq_swap(j).wait_send()

        @pl.when(pipe > 0)
        def _():
            for column in range(2):
                hand_back(j, column).wait_send()

        @pl.when(pipe < 15)
        def _():
            for column in range(2):
                hand_back(j, column).wait_recv()

        for t in range(2):
            for d in range(SLOTS):
                @pl.when(d + 1 <= chain_above)
                def _():
                    if j == 0 and d == 0:
                        for column in range(2):
                            first_up(t, column).wait_send()
                    else:
                        up(j, d, t).wait_send()

                if d >= 1:
                    @pl.when((d <= chain) & (z >= 3))
                    def _():
                        down(j, d, t).wait_send()

                if d == 1 or d == 2:
                    @pl.when((d <= chain) & (z <= 2))
                    def _():
                        down_wide(j, d, t).wait_send()

            @pl.when(z <= 3)
            def _():
                round_first(j, t).wait_send()

            @pl.when(z == 1)
            def _():
                round_on(j, t).wait_send()
                extra_on(j, t).wait_send()

            for e in range(2):
                @pl.when(z == 7)
                def _():
                    extra(j, e, t).wait_send()

                @pl.when(last_block)
                def _():
                    extra_back(j, e, t, above, e).wait_send()

            @pl.when(z == 7)
            def _():
                extra_back(j, 0, t, level(2), 2).wait_send()

    for t in range(2):
        stat_swap(t).wait_send()


def write_out(*refs):
    done = refs[12]

    def piece(stage, i, c):
        part = pl.ds(c * 64, 64)
        return pltpu.make_async_copy(
            refs[(i, 8 + i)[stage]].at[0, part], refs[(8 + i, 4 + i)[stage]].at[0, part],
            done.at[stage, i, c],
        )

    pieces = [(i, c) for i in (0, 3, 1, 2) for c in range(2)]
    for i, c in pieces:
        piece(0, i, c).start()
    for i, c in pieces:
        piece(0, i, c).wait()
        piece(1, i, c).start()
    for i, c in pieces:
        piece(1, i, c).wait()


def per_device(queries, key_heads, value_heads, out_grad, log_sum, row_delta, chosen):
    vmem = pl.BlockSpec(memory_space=pltpu.VMEM)
    hbm = pl.BlockSpec(memory_space=pltpu.HBM)
    dma = pltpu.SemaphoreType.DMA
    level = (2, PAIR, HD)
    flops = 5 * 2 * ROWS * H * HD * 1536
    grads = pl.pallas_call(
        kernel,
        out_shape=(
            jax.ShapeDtypeStruct(queries.shape, BF16),
            jax.ShapeDtypeStruct(key_heads.shape, BF16),
            jax.ShapeDtypeStruct(value_heads.shape, BF16),
            jax.ShapeDtypeStruct(queries.shape, BF16),
        ),
        in_specs=[pl.BlockSpec(memory_space=pltpu.SMEM)] + [hbm] * 6,
        out_specs=(vmem,) * 4,
        scratch_shapes=[
            pltpu.VMEM((2, ROWS, 2048), BF16),
            pltpu.VMEM((2, ROWS, 2048), BF16),
            pltpu.VMEM((2, SLOTS) + level, BF16),
            pltpu.VMEM((2, 4) + level, BF16),
            pltpu.VMEM((2, SLOTS) + level, F32),
            pltpu.VMEM((2, HD, 2048), F32),
            pltpu.VMEM((2, 2, 16, ROWS), F32),
            pltpu.VMEM((2, 2, 16, ROWS), BF16),
            pltpu.VMEM((2, SLOTS) + level, BF16),
            pltpu.VMEM((2, SLOTS) + level, BF16),
            pltpu.VMEM((2, 2) + level, F32),
            pltpu.VMEM((2, 2) + level, F32),
            pltpu.VMEM((2, 2) + level, BF16),
            pltpu.VMEM((2, 2) + level, BF16),
            pltpu.VMEM((2, ROWS, 1024), BF16),
            pltpu.VMEM((2,) + level, BF16),
            dma((5, 2)),
            dma((3, 2)), dma((3, 2)),
            dma((2, 2)), dma((2, 2)),
            dma((2, 2)),
            dma((2, SLOTS, 2)), dma((2, SLOTS, 2)),
            dma((2, 2, 2)), dma((2, 4, 2)),
            dma((2, 2, 2)), dma((2, 2, 2)),
            dma((2, SLOTS, 2)), dma((2, SLOTS, 2)),
            dma((2, 3, 2)), dma((2, 2, 2)),
            dma((2,)), dma((2,)),
            dma((2, 2)), dma((2, 2)),
            dma((2, 2)), dma((2, 2)),
        ],
        compiler_params=pltpu.CompilerParams(
            collective_id=0, has_side_effects=True, vmem_limit_bytes=63 * 2**20
        ),
        cost_estimate=pl.CostEstimate(
            flops=flops, bytes_accessed=6 * 2**20, transcendentals=ROWS * H * 1536
        ),
        name="block_attention_backward",
    )(chosen.transpose(0, 2, 1), queries, key_heads, value_heads, out_grad, log_sum, row_delta)
    anywhere = pl.BlockSpec(memory_space=pl.ANY)
    return pl.pallas_call(
        write_out,
        out_shape=tuple(jax.ShapeDtypeStruct(part.shape, part.dtype) for part in grads),
        in_specs=[anywhere] * 4,
        out_specs=(anywhere,) * 4,
        scratch_shapes=[pltpu.VMEM(part.shape, part.dtype) for part in grads] + [dma((2, 4, 2))],
        name="write_out",
    )(*grads)


def solution(mesh):
    heads = P("pipe", "ctx", None)
    stats = P("pipe", None, "ctx")
    return jax.shard_map(
        per_device,
        mesh=mesh,
        in_specs=(heads, heads, heads, heads, stats, stats, P("pipe", None, None)),
        out_specs=(heads, heads, heads, heads),
        check_vma=False,
    )
```
